32 devices in a mesh: panel: 2 (over x), lat: 2 (over y), lon: 8 (over z, core).
Axes of the slice: x: 2, y: 2, z: 4, core: 2. Of those that a mesh axis runs over, the one named last changes fastest.
Arguments:
- fields: float32 [2, 6, 4, 256, 1024], P('panel', None, None, 'lat', 'lon'), may hold values from -6 to 6
- viscosity: float32 [2, 4, 256, 1024], P('panel', None, 'lat', 'lon'), may hold values from 0.01 to 0.1
- partner: int32 [2, 2, 64, 1], P('panel', 'lat', 'lon'), may hold values from 0 to 7; in each aligned block of 8 rows (0 to 7, 8 to 15, ..., all dimensions but the last counted through in order) at most 2 rows name the same one
- src_row: int32 [2, 2, 4096], P('panel', 'lat', 'lon'), may hold values from 0 to 126
- src_col: int32 [2, 2, 4096], P('panel', 'lat', 'lon'), may hold values from 0 to 126
- weight_id: int32 [2, 2, 4096], P('panel', 'lat', 'lon'), may hold values from 0 to 63
- border_angle: float32 [2, 2, 4096], P('panel', 'lat', 'lon'), may hold values from -3.140625 to 3.140625
- dest_cell: int32 [2, 2, 4096], P('panel', 'lat', 'lon'), may hold values from 0 to 16383, as said below
Outputs:
- new_fields: float32 [2, 6, 4, 256, 1024], P('panel', None, None, 'lat', 'lon')
- pressure: float32 [2, 4, 256, 1024], P('panel', None, 'lat', 'lon')
The draws below stay inside these ranges and needn't reach their ends.
Inputs may be any that keep to these rules, and one draw needn't show every extreme that they name: `partner`: A border block's sources lie on the device of the other panel with the same lat index and this lon index; among the 8 blocks of one device no lon index is named by more than 2 blocks. `dest_cell`: the 512 border cells of one device are distinct cells of its block.
All inputs are finite; a program needn't handle non-finite values.
Results may differ from the reference program's by a relative error of at most 0.0002.
Values sent between devices are 32-bit elements; how exact they have to be, the bound alone decides.
A program may use at most 128 MiB of HBM per device.

```python
import math
import jax
import jax.numpy as jnp
import numpy as np
from jax import lax

NR = 4
CLAT = 128
CLON = 128
BC = 64
CAP = 2
WQ = 8
NB = 8
NTH = 256
NPH = 1024
N_LAT = 2
N_LON = 8


def draw_dest_cell(key, part):
    devices = 2 * N_LAT * N_LON
    key_list = jax.random.split(key, devices)
    orders = jax.vmap(lambda sub_key: jax.random.permutation(sub_key, CLAT * CLON))(key_list)
    return orders[:, :NB * BC].astype(jnp.int32).reshape(2, N_LAT, N_LON * NB * BC)


def place_ends(entries, key, low, high):
    shape = entries.shape
    index_at = [jax.random.randint(jax.random.fold_in(key, axis), (), 0, shape[axis]) for axis in range(len(shape))]
    entries = entries.at[tuple(index_at)].set(low)
    longest = shape.index(max(shape))
    index_at[longest] = (index_at[longest] + 1) % shape[longest]
    return entries.at[tuple(index_at)].set(high)


def level_of(stream_key, shape, cuts, least, largest):
    level = 1.0
    for axis_at, parts in cuts:
        heights = jax.random.uniform(jax.random.fold_in(jax.random.fold_in(stream_key, 6), axis_at), (parts,), jnp.float32, least / len(cuts), largest / len(cuts))
        level = level * jnp.repeat(jnp.exp(heights), shape[axis_at] // parts).reshape((-1,) + (1,) * (len(shape) - 1 - axis_at))
    return level


def routed_block(stream_key, own, number, rows, count, top, limit, skew):
    ranking = jax.random.permutation(stream_key, count)
    crowded, common = portions_of(count, rows * top, limit, skew, True), portions_of(count, rows * top, limit, skew, False)
    places = jnp.arange(count)

    def named(lengths, turn):
        used = int((lengths > 0).sum())
        fixed = max(1, used // 4)
        moved = fixed + (places - fixed + turn * (used - fixed)) % max(1, count - fixed)
        return jnp.zeros((count,), jnp.int32).at[ranking[jnp.where(places < fixed, places, moved)]].set(jnp.asarray(lengths, jnp.int32))

    lengths = jnp.where(number % 4 == 0, named(crowded, number // 4), named(common, number - number // 4 - 1))
    mixed = jax.random.permutation(jax.random.fold_in(own, 3), count)
    source_of, sink = mixed[0:count // 2 * 2:2], mixed[1:count // 2 * 2:2]
    margin = jnp.minimum(lengths[source_of] - 1, limit - lengths[sink]) // 2
    margin = jnp.where((source_of == ranking[0]) | (sink == ranking[0]) | (lengths[sink] == 0), 0, jnp.maximum(margin, 0))
    moved = jax.random.randint(jax.random.fold_in(own, 4), (count // 2,), 0, 1 << 20) % (margin + 1)
    lengths = lengths.at[source_of].add(-moved).at[sink].add(moved)
    items = jnp.searchsorted(jnp.cumsum(lengths), jnp.arange(rows * top), side="right").astype(jnp.int32)
    grid = items.reshape(top, rows).T
    grid = grid[jax.random.permutation(jax.random.fold_in(own, 1), rows)]
    turn = jax.random.randint(jax.random.fold_in(own, 2), (rows, 1), 0, top)
    return jnp.take_along_axis(grid, (jnp.arange(top)[None, :] + turn) % top, axis=1)


def portions_of(amount, total, bound, skew, full):
    weights = [(1 << 20) // math.isqrt(rank ** skew) + 1 for rank in range(1, amount + 1)]
    largest = bound if full else min(bound, max(-(-total // amount), total * weights[0] // sum(weights)))
    least = 1 if total - largest >= amount - 1 else 0
    holding, spare = [largest] + [least] * (amount - 1), total - largest - least * (amount - 1)
    while spare > 0:
        movable = [i for i in range(1, amount) if holding[i] < largest] or [i for i in range(1, amount) if holding[i] < bound]
        whole, left = sum([weights[i] for i in movable]), spare
        for i in movable:
            addition = min(bound - holding[i], max(1, left * weights[i] // whole), spare)
            holding[i] = holding[i] + addition
            spare = spare - addition
    return np.array(holding)


def bell_draw(rng, extent, deviation, limit, shards=(), kind=jnp.bfloat16):
    entries = jax.random.normal(rng, extent, jnp.float32) * deviation
    if len(shards) > 0:
        entries = level_of(rng, extent, shards, -0.22, 0.18) * entries
    return jnp.clip(entries, min=-limit, max=limit).astype(kind)


def setup_inputs(seed: int = 0) -> dict:
    key_of = jax.random.split(jax.random.key(seed), 9)
    fields = bell_draw(key_of[0], (2, 6, NR, NTH, NPH), 1.0, 6.0, ((0, 2), (3, 2), (4, 8)), jnp.float32)
    viscosity = jnp.clip(jnp.exp(math.log(0.1) - 2.3025851 * jax.random.uniform(key_of[1], (2, NR, NTH, NPH), jnp.float32) ** level_of(key_of[1], (2, NR, NTH, NPH), ((0, 2), (2, 2), (3, 8)), -0.2, 0.2)), 0.01, 0.1)
    partner_keys = jax.random.split(jax.random.fold_in(key_of[2], 1), 2 * N_LAT * (N_LON * NB) // NB)
    partner_turns = jax.random.permutation(jax.random.fold_in(key_of[2], 3), 2 * N_LAT * (N_LON * NB) // NB)
    partner = jax.vmap(lambda own, number: routed_block(jax.random.fold_in(key_of[2], 2), own, number, NB, N_LON, 1, CAP, 1))(partner_keys, partner_turns).reshape((2, N_LAT, N_LON * NB, 1))
    src_row = place_ends(jax.random.randint(key_of[3], (2, N_LAT, N_LON * NB * BC), 0, CLAT - 1), jax.random.fold_in(key_of[3], 1), 0, (CLAT - 1) - 1).astype(jnp.int32)
    src_col = place_ends(jax.random.randint(key_of[4], (2, N_LAT, N_LON * NB * BC), 0, CLON - 1), jax.random.fold_in(key_of[4], 1), 0, (CLON - 1) - 1).astype(jnp.int32)
    weight_id = place_ends(jax.random.randint(key_of[5], (2, N_LAT, N_LON * NB * BC), 0, WQ * WQ), jax.random.fold_in(key_of[5], 1), 0, (WQ * WQ) - 1).astype(jnp.int32)
    border_angle = jnp.clip(jax.random.uniform(key_of[6], (2, N_LAT, N_LON * NB * BC), jnp.float32, -3.140625, 3.140625), -3.140625, 3.140625)
    dest_cell = draw_dest_cell(jax.random.fold_in(key_of[8], 71), 0)
    return {"fields": fields, "viscosity": viscosity, "partner": partner, "src_row": src_row, "src_col": src_col, "weight_id": weight_id, "border_angle": border_angle, "dest_cell": dest_cell}


BUOYANCY = 0.5

def metric(row_index, total_rows):
    colatitude = math.pi / 4.0 + (row_index.astype(jnp.float32) + 0.5) * (math.pi / 2.0) / total_rows
    inv_sine = 1.0 / jnp.sin(colatitude)
    return (inv_sine, inv_sine * inv_sine)

def lap_shrink(field, row_gain):
    centre = field[..., 1:-1, 1:-1]
    padded = jnp.pad(centre, [(0, 0)] * (centre.ndim - 3) + [(1, 1), (0, 0), (0, 0)])
    lat_term = field[..., 2:, 1:-1] + field[..., :-2, 1:-1] - 2.0 * centre
    lon_term = field[..., 1:-1, 2:] + field[..., 1:-1, :-2] - 2.0 * centre
    radial = padded[..., 2:, :, :] + padded[..., :-2, :, :] - 2.0 * centre
    return lat_term + row_gain[:, None] * lon_term + radial

def diverge(velocity, inv_sine):
    radial_pad = jnp.pad(velocity[0, :, 1:-1, 1:-1], ((1, 1), (0, 0), (0, 0)))
    lat_part = velocity[1, :, 2:, 1:-1] - velocity[1, :, :-2, 1:-1]
    lon_part = velocity[2, :, 1:-1, 2:] - velocity[2, :, 1:-1, :-2]
    rad_part = radial_pad[2:] - radial_pad[:-2]
    return 0.5 * (lat_part + inv_sine[:, None] * lon_part + rad_part)

def gradient(pressure, inv_sine):
    radial_pad = jnp.pad(pressure[:, 1:-1, 1:-1], ((1, 1), (0, 0), (0, 0)))
    grad_rad = 0.5 * (radial_pad[2:] - radial_pad[:-2])
    grad_lat = 0.5 * (pressure[:, 2:, 1:-1] - pressure[:, :-2, 1:-1])
    grad_lon = 0.5 * inv_sine[:, None] * (pressure[:, 1:-1, 2:] - pressure[:, 1:-1, :-2])
    return (grad_rad, grad_lat, grad_lon)

def cosine_table(length):
    mode_ids = jnp.arange(length, dtype=jnp.float32)
    cell_mid = jnp.arange(length, dtype=jnp.float32) + 0.5
    row_norm = jnp.sqrt(jnp.where(mode_ids > 0, 2.0, 1.0) / length)
    cos_table = row_norm[:, None] * jnp.cos(math.pi * mode_ids[:, None] * cell_mid[None, :] / length)
    eigenvalue = 4.0 * jnp.sin(math.pi * mode_ids / (2.0 * length)) ** 2
    return (cos_table, eigenvalue)

def coarse_divisor(levels, n_lat, n_lon):
    eig_rad = cosine_table(levels)[1]
    eig_lat = cosine_table(n_lat)[1]
    eig_lon = cosine_table(n_lon)[1]
    return eig_rad[:, None, None] + eig_lat[None, :, None] + eig_lon[None, None, :] + 1.0 / (n_lat * n_lon)

def coarse_solve(block_sum, n_lat, n_lon):
    highest = lax.Precision.HIGHEST
    tab_rad = cosine_table(block_sum.shape[0])[0]
    tab_lat = cosine_table(n_lat)[0]
    tab_lon = cosine_table(n_lon)[0]
    spectrum = jnp.einsum('kr,rlo->klo', tab_rad, block_sum, precision=highest)
    spectrum = jnp.einsum('kl,rlo->rko', tab_lat, spectrum, precision=highest)
    spectrum = jnp.einsum('ko,rlo->rlk', tab_lon, spectrum, precision=highest)
    spectrum = spectrum / coarse_divisor(block_sum.shape[0], n_lat, n_lon)
    restored = jnp.einsum('kr,klo->rlo', tab_rad, spectrum, precision=highest)
    restored = jnp.einsum('kl,rko->rlo', tab_lat, restored, precision=highest)
    restored = jnp.einsum('ko,rlk->rlo', tab_lon, restored, precision=highest)
    return restored / math.sqrt(n_lat * n_lon)

def fractions(weight_ids):
    frac_lat = ((weight_ids // WQ).astype(jnp.float32) + 0.5) / WQ
    frac_lon = ((weight_ids % WQ).astype(jnp.float32) + 0.5) / WQ
    return (frac_lat, frac_lon)

def bilinear(lower_left, lower_right, upper_left, upper_right, frac_lat, frac_lon):
    return (1.0 - frac_lat) * (1.0 - frac_lon) * lower_left + (1.0 - frac_lat) * frac_lon * lower_right + frac_lat * (1.0 - frac_lon) * upper_left + frac_lat * frac_lon * upper_right

def reference(fields, viscosity, partner, src_row, src_col, weight_id, border_angle, dest_cell):
    n_lat, n_lon = (N_LAT, N_LON)
    total_rows, total_cols = (CLAT * n_lat, CLON * n_lon)
    channels = 6 * NR
    cells = jnp.transpose(fields.reshape(2, channels, total_rows, total_cols), (0, 2, 3, 1))
    shape = (2, n_lat, n_lon, NB, BC)
    panel_ids = jnp.arange(2, dtype=jnp.int32).reshape(2, 1, 1, 1, 1)
    lat_ids = jnp.arange(n_lat, dtype=jnp.int32).reshape(1, n_lat, 1, 1, 1)
    lon_ids = jnp.arange(n_lon, dtype=jnp.int32).reshape(1, 1, n_lon, 1, 1)
    target = partner.reshape(2, n_lat, n_lon, NB, 1)
    other = jnp.broadcast_to(1 - panel_ids, shape)
    src_lat = jnp.broadcast_to(lat_ids * CLAT + src_row.reshape(shape), shape)
    src_lon = jnp.broadcast_to(target * CLON + src_col.reshape(shape), shape)
    lower_left = cells[other, src_lat, src_lon]
    lower_right = cells[other, src_lat, src_lon + 1]
    upper_left = cells[other, src_lat + 1, src_lon]
    upper_right = cells[other, src_lat + 1, src_lon + 1]
    frac_lat, frac_lon = fractions(weight_id.reshape(shape))
    values = bilinear(lower_left, lower_right, upper_left, upper_right, frac_lat[..., None], frac_lon[..., None])
    values = values.reshape(shape + (6, NR))
    turn = border_angle.reshape(shape)[..., None]
    cos_angle = jnp.cos(turn)
    sin_angle = jnp.sin(turn)
    rotated = jnp.stack([values[..., 0, :], cos_angle * values[..., 1, :] + sin_angle * values[..., 2, :], cos_angle * values[..., 2, :] - sin_angle * values[..., 1, :], values[..., 3, :], cos_angle * values[..., 4, :] + sin_angle * values[..., 5, :], cos_angle * values[..., 5, :] - sin_angle * values[..., 4, :]], axis=-2).reshape(shape + (channels,))
    dest = dest_cell.reshape(shape)
    dest_lat = jnp.broadcast_to(lat_ids * CLAT + dest // CLON, shape)
    dest_lon = jnp.broadcast_to(lon_ids * CLON + dest % CLON, shape)
    cells = cells.at[jnp.broadcast_to(panel_ids, shape), dest_lat, dest_lon].set(rotated)
    filled = jnp.transpose(cells, (0, 3, 1, 2)).reshape(2, 6, NR, total_rows, total_cols)
    row_index = jnp.arange(total_rows, dtype=jnp.int32)
    inv_sine, row_gain = metric(row_index, total_rows)
    rim_four = ((0, 0), (0, 0), (1, 1), (1, 1))
    rim_three = ((0, 0), (1, 1), (1, 1))
    outputs = []
    pressures = []
    for panel in range(2):
        current = filled[panel]
        stepped = current + viscosity[panel][None] * lap_shrink(jnp.pad(current, rim_four), row_gain)
        stepped = jnp.concatenate([stepped[0:1] + BUOYANCY * current[3:4], stepped[1:]], axis=0)
        divergence = diverge(jnp.pad(stepped[0:3], rim_four), inv_sine)
        press_one = -divergence / (4.0 + 2.0 * row_gain)[:, None]
        resid_one = -divergence + lap_shrink(jnp.pad(press_one, rim_three), row_gain)
        block_sum = resid_one.reshape(NR, n_lat, CLAT, n_lon, CLON).sum(axis=(2, 4)) * (1.0 / math.sqrt(CLAT * CLON))
        coarse = coarse_solve(block_sum, n_lat, n_lon)
        pressure = press_one + jnp.repeat(jnp.repeat(coarse, CLAT, axis=1), CLON, axis=2)
        grad_rad, grad_lat, grad_lon = gradient(jnp.pad(pressure, rim_three), inv_sine)
        outputs.append(jnp.stack([stepped[0] - grad_rad, stepped[1] - grad_lat, stepped[2] - grad_lon, stepped[3], stepped[4], stepped[5]], axis=0))
        pressures.append(pressure)
    return (jnp.stack(outputs, axis=0), jnp.stack(pressures, axis=0))
```

```python
import functools
import math

import jax
import jax.numpy as jnp
import numpy as np
from jax import lax
from jax.experimental import pallas as pl
from jax.experimental.pallas import tpu as pltpu
from jax.sharding import PartitionSpec as P

MESH = pl.DeviceIdType.MESH
WQ = 8
BUOYANCY = 0.5
TOP = 8
F32 = jnp.float32
BF16 = jnp.bfloat16


def coarse_operator(levels, n_lat, n_lon):
    def table(n):
        m = np.arange(n, dtype=np.float64)
        norm = np.sqrt(np.where(m > 0, 2.0, 1.0) / n)
        q = norm[:, None] * np.cos(np.pi * m[:, None] * (m[None, :] + 0.5) / n)
        return q, 4.0 * np.sin(np.pi * m / (2.0 * n)) ** 2

    qr, er = table(levels)
    qa, ea = table(n_lat)
    qo, eo = table(n_lon)
    inv = 1.0 / (
        ea[:, None, None] + eo[None, :, None] + er[None, None, :] + 1.0 / (n_lat * n_lon)
    )
    q = np.einsum("ax,oy,rz->aorxyz", qa, qo, qr).reshape(inv.size, inv.size)
    full = (q.T * inv.reshape(-1)) @ q / math.sqrt(n_lat * n_lon)
    count = inv.size
    wide = np.zeros((count, 8 * 128), np.float32)
    wide[:, :count] = full
    return wide.reshape(n_lat * n_lon, levels, 8, 128)


def windows(levels):
    spans, at = [], 0
    for width in (3, 3, 3, 2, 1, 1):
        for _ in range(levels):
            spans.append((at + width, width))
            at += 2 * width
    return spans


def visc_windows(levels):
    return [(4 * k + 2, 2) for k in range(levels)]


def pack(tiles, spans, lane):
    packed = None
    for tile, (centre, width) in zip(tiles, spans):
        moved = pltpu.roll(tile, centre, 1)
        inside = (lane >= centre - width) & (lane < centre + width)
        packed = jnp.where(inside, moved, 0.0 if packed is None else packed)
    return packed


def right_part(spans, lane):
    mask = jnp.zeros(lane.shape, jnp.int32)
    for centre, width in spans:
        mask = jnp.where((lane >= centre) & (lane < centre + width), 1, mask)
    return mask > 0


def unpack(merged, span, lane):
    centre, width = span
    moved = pltpu.roll(merged, (128 - centre) % 128, 1)
    return jnp.where((lane < width) | (lane >= 128 - width), moved, 0.0)


def kernel(
    dims,
    partner_ref, row_ref, col_ref, wid_ref, ang_ref, dest_ref, fields_ref, visc_ref, oper_ref,
    out_ref, press_ref,
    fld, fcat, ask, asked, reply, answer, x, hx, pk, pkl, pkr, va, vh, vpk, vpl, vpr,
    inv_s, gain_s, coef_a, coef_h, st, sth, p1, p1h, hit_s, rmask, cmask,
    opr, sums, mine, onew, opress,
    in_sem, op_sem, out_sem, ask_send, ask_recv, rep_send, rep_recv,
    halo_send, halo_recv, v_send, v_recv, sum_send, sum_recv,
):
    n_lat, n_lon, levels, blocks = dims
    ndev = n_lat * n_lon
    channels = 6 * levels
    rows_ext = 128 + 2 * TOP
    pairs = blocks // 2
    cells = blocks * 64
    p = lax.axis_index("panel")
    a = lax.axis_index("lat")
    b = lax.axis_index("lon")
    me = a * n_lon + b
    own = pl.ds(TOP, 128)

    def dev(panel, lat, lon):
        return {"panel": panel, "lat": lat, "lon": lon}

    load_f = pltpu.make_async_copy(fields_ref.at[0], fld, in_sem.at[0])
    load_v = pltpu.make_async_copy(visc_ref.at[0], va.at[:, own, :], in_sem.at[1])
    load_f.start()
    load_v.start()
    targets = (
        me,
        jnp.maximum(a - 1, 0) * n_lon + b,
        jnp.minimum(a + 1, n_lat - 1) * n_lon + b,
        a * n_lon + jnp.maximum(b - 1, 0),
        a * n_lon + jnp.minimum(b + 1, n_lon - 1),
    )
    load_o = [
        pltpu.make_async_copy(oper_ref.at[t], opr.at[i], op_sem.at[i])
        for i, t in enumerate(targets)
    ]
    for c in load_o:
        c.start()

    barrier = pltpu.get_barrier_semaphore()

    def greet(i, carry):
        t = lax.rem(me + i, ndev)
        pl.semaphore_signal(
            barrier, inc=1, device_id=dev(p, t // n_lon, lax.rem(t, n_lon)), device_id_type=MESH
        )
        return carry

    lax.fori_loop(1, ndev, greet, 0)

    def greet_other(i, carry):
        pl.semaphore_signal(barrier, inc=1, device_id=dev(1 - p, a, i), device_id_type=MESH)
        return carry

    lax.fori_loop(0, n_lon, greet_other, 0)

    lane8 = lax.broadcasted_iota(jnp.int32, (8, 128), 1)
    sub8 = lax.broadcasted_iota(jnp.int32, (8, 128), 0)
    half = lane8 // 64
    pv = jnp.broadcast_to(partner_ref[0, 0], (blocks, 128))
    block_id = lax.broadcasted_iota(jnp.int32, (blocks, 128), 0)
    before = jnp.zeros((blocks, 128), jnp.int32)
    for k in range(blocks):
        before = before + jnp.where((pv == pv[k : k + 1]) & (block_id > k), 1, 0)
    slot = pv * 2 + before
    keys, keys_r, tiles, tiles_r = [], [], [], []
    for j in range(pairs):
        s0 = jnp.broadcast_to(slot[2 * j : 2 * j + 1], (8, 128))
        s1 = jnp.broadcast_to(slot[2 * j + 1 : 2 * j + 2], (8, 128))
        key = jnp.where(half == 0, s0, s1)
        at = pl.ds(128 * j, 128)
        rr = jnp.broadcast_to(row_ref[0, :, at], (8, 128))
        cc = jnp.broadcast_to(col_ref[0, :, at], (8, 128))
        ww = jnp.broadcast_to(wid_ref[0, :, at], (8, 128))
        tile = jnp.where(sub8 == 0, rr, jnp.where(sub8 == 1, cc, ww))
        keys.append(key)
        tiles.append(tile)
        keys_r.append(pltpu.roll(key, 64, 1))
        tiles_r.append(pltpu.roll(tile, 64, 1))
    for q in range(n_lon):
        want = 2 * q + half
        acc = jnp.zeros((8, 128), jnp.int32)
        for j in range(pairs):
            acc = jnp.where(keys[j] == want, tiles[j], acc)
            acc = jnp.where(keys_r[j] == want, tiles_r[j], acc)
        ask[q] = acc

    pl.semaphore_wait(barrier, ndev - 1 + n_lon)

    def ask_copy(q, there):
        return pltpu.make_async_remote_copy(
            src_ref=ask.at[q], dst_ref=asked.at[there],
            send_sem=ask_send.at[q], recv_sem=ask_recv.at[there],
            device_id=dev(1 - p, a, q), device_id_type=MESH,
        )

    def send_ask(i, carry):
        q = lax.rem(b + i, n_lon)
        ask_copy(q, b).start()
        return carry

    lax.fori_loop(0, n_lon, send_ask, 0)

    ways = [(da, db) for da in (-1, 0, 1) for db in (-1, 0, 1) if (da, db) != (0, 0)]

    def exists(da, db):
        ok = None
        for pos, d, n in ((a, da, n_lat), (b, db, n_lon)):
            if d:
                c = (pos > 0) if d < 0 else (pos < n - 1)
                ok = c if ok is None else jnp.logical_and(ok, c)
        return ok

    def halo_copy(w, body, packed, from_left, from_right, send, recv):
        da, db = ways[w]
        src_rows = {-1: pl.ds(0, TOP), 0: pl.ds(0, 128), 1: pl.ds(128 - TOP, TOP)}[da]
        dst_rows = {-1: pl.ds(TOP + 128, TOP), 0: own, 1: pl.ds(0, TOP)}[da]
        if db == 0:
            src = body.at[:, pl.ds(TOP if da < 0 else 128, TOP), :]
            dst = body.at[:, dst_rows, :]
        else:
            src = packed.at[src_rows, :]
            dst = (from_left if db > 0 else from_right).at[dst_rows, :]
        return pltpu.make_async_remote_copy(
            src_ref=src, dst_ref=dst, send_sem=send.at[w], recv_sem=recv.at[w],
            device_id=dev(p, a + da, b + db), device_id_type=MESH,
        )

    def halo_send_all(*args):
        for w in range(8):
            @pl.when(exists(*ways[w]))
            def _(w=w):
                halo_copy(w, *args).start()

    def halo_wait_recv(*args):
        for w in range(8):
            da, db = ways[w]

            @pl.when(exists(-da, -db))
            def _(w=w):
                halo_copy(w, *args).wait_recv()

    def halo_wait_send(*args):
        for w in range(8):
            @pl.when(exists(*ways[w]))
            def _(w=w):
                halo_copy(w, *args).wait_send()

    def halo_clear(body, from_left, from_right):
        for w in range(8):
            da, db = ways[w]
            dst_rows = {-1: pl.ds(TOP + 128, TOP), 0: own, 1: pl.ds(0, TOP)}[da]

            @pl.when(jnp.logical_not(exists(-da, -db)))
            def _(da=da, db=db, dst_rows=dst_rows):
                if db == 0:
                    body[:, dst_rows, :] = jnp.zeros((body.shape[0], TOP, 128), F32)
                else:
                    buf = from_left if db > 0 else from_right
                    n = 128 if da == 0 else TOP
                    buf[dst_rows, :] = jnp.zeros((n, 128), F32)

    lane = lax.broadcasted_iota(jnp.int32, (rows_ext, 128), 1)
    lane_o = lax.broadcasted_iota(jnp.int32, (128, 128), 1)
    row_e = lax.broadcasted_iota(jnp.int32, (rows_ext, 128), 0)

    vargs = (va, vpk, vpl, vpr, v_send, v_recv)
    xargs = (x, pk, pkl, pkr, halo_send, halo_recv)
    halo_clear(va, vpl, vpr)
    load_v.wait()
    vpk[...] = pack([va[k, own, :] for k in range(levels)], visc_windows(levels), lane_o)
    halo_send_all(*vargs)
    halo_clear(x, pkl, pkr)

    load_f.wait()
    for f in range(6):
        v = fld[f].reshape(levels * 128, 128)
        hi = v.astype(BF16)
        lo = (v - hi.astype(F32)).astype(BF16)
        fcat[f, :, 0:128] = hi
        fcat[f, :, 128:256] = lo

    def rep_copy(q, there):
        return pltpu.make_async_remote_copy(
            src_ref=reply.at[q], dst_ref=answer.at[there],
            send_sem=rep_send.at[q], recv_sem=rep_recv.at[there],
            device_id=dev(1 - p, a, q), device_id_type=MESH,
        )

    sub_c = lax.broadcasted_iota(jnp.int32, (128, 256), 0)

    def serve(i, carry):
        pr = lax.rem(b // 2 + i, n_lon // 2)
        q0 = 2 * pr
        ask_copy(0, q0).wait_recv()
        ask_copy(0, q0 + 1).wait_recv()
        r0 = asked[q0]
        r1 = asked[q0 + 1]
        rr = jnp.concatenate([r0[0:1], r1[0:1]], axis=1)
        cc = jnp.concatenate([r0[1:2], r1[1:2]], axis=1)
        ww = jnp.concatenate([r0[2:3], r1[2:3]], axis=1)
        fa = ((ww >> 3).astype(F32) + 0.5) / WQ
        fo = ((ww & 7).astype(F32) + 0.5) / WQ
        cw = jnp.where(sub_c == cc, 1.0 - fo, jnp.where(sub_c == cc + 1, fo, 0.0)).astype(BF16)
        rw = jnp.where(sub_c == rr, 1.0 - fa, jnp.where(sub_c == rr + 1, fa, 0.0))
        cw2 = jnp.concatenate([cw, cw], axis=0)
        parts = []
        for f in range(6):
            g = jnp.dot(fcat[f], cw2, preferred_element_type=F32)
            parts.append(jnp.sum(g.reshape(levels, 128, 256) * rw[None], axis=1))
        res = jnp.concatenate(parts, axis=0)
        reply[q0] = res[:, 0:128]
        reply[q0 + 1] = res[:, 128:256]
        rep_copy(q0, b).start()
        rep_copy(q0 + 1, b).start()
        return carry

    lax.fori_loop(0, n_lon // 2, serve, 0)

    dest = dest_ref[0]
    sub_d = lax.broadcasted_iota(jnp.int32, (128, cells), 0)
    rm = jnp.where(sub_d == dest // 128, 1.0, 0.0).astype(BF16)
    cm = jnp.where(sub_d == dest % 128, 1.0, 0.0).astype(BF16)
    rmask[...] = rm
    cmask[:, 0:cells] = cm
    cmask[:, cells : 2 * cells] = cm
    nt = (((1,), (1,)), ((), ()))
    hit_s[...] = lax.dot_general(rm, cm, nt, preferred_element_type=F32)
    cos_a = jnp.cos(ang_ref[0])
    sin_a = jnp.sin(ang_ref[0])
    colat = math.pi / 4.0 + ((a * 128 + row_e - TOP).astype(F32) + 0.5) * (
        math.pi / 2.0
    ) / (n_lat * 128)
    inv = 1.0 / jnp.sin(colat)
    gain = inv * inv
    inv_s[...] = inv
    gain_s[...] = gain
    is_own = (row_e >= TOP) & (row_e < TOP + 128)
    edge_lane = (lane == 0) | (lane == 127)
    ca = 2.0 + 2.0 * gain
    ca = ca - jnp.where((row_e == TOP) | (row_e == TOP + 127), 1.0, 0.0)
    ca = ca - jnp.where(edge_lane, gain, 0.0)
    rim = jnp.where((row_e == TOP - 1) | (row_e == TOP + 128), 1.0, 0.0)
    coef_a[...] = jnp.where(is_own, ca, rim)
    coef_h[...] = jnp.where(is_own & edge_lane, gain, 0.0)
    halo_wait_recv(*vargs)
    vmerged = jnp.where(right_part(visc_windows(levels), lane), vpr[...], vpl[...])
    for k in range(levels):
        vh[k] = unpack(vmerged, visc_windows(levels)[k], lane)

    def wait_rep(q, carry):
        rep_copy(0, q).wait_recv()
        return carry

    lax.fori_loop(0, n_lon, wait_rep, 0)
    got = [answer[q] for q in range(n_lon)]
    got_r = [pltpu.roll(g, 64, 1) for g in got]
    half_row = half[0:1]
    picked = []
    for j in range(pairs):
        key = keys[j][0:1]
        acc = jnp.zeros((channels, 128), F32)
        for q in range(n_lon):
            acc = jnp.where(key == 2 * q + half_row, got[q], acc)
            acc = jnp.where(key == 2 * q + 1 - half_row, got_r[q], acc)
        picked.append(acc)
    values = jnp.concatenate(picked, axis=1)
    fv = [values[f * levels : (f + 1) * levels] for f in range(6)]
    turned = [
        fv[0],
        cos_a * fv[1] + sin_a * fv[2],
        cos_a * fv[2] - sin_a * fv[1],
        fv[3],
        cos_a * fv[4] + sin_a * fv[5],
        cos_a * fv[5] - sin_a * fv[4],
    ]
    hit = hit_s[...] > 0.5
    for f in range(6):
        hi = turned[f].astype(BF16)
        lo = (turned[f] - hi.astype(F32)).astype(BF16)
        left = []
        for k in range(levels):
            left.append(
                jnp.concatenate(
                    [rmask[...] * hi[k : k + 1], rmask[...] * lo[k : k + 1]], axis=1
                )
            )
        put = lax.dot_general(
            jnp.concatenate(left, axis=0), cmask[...], nt, preferred_element_type=F32
        )
        for k in range(levels):
            x[f * levels + k, own, :] = jnp.where(
                hit, put[k * 128 : (k + 1) * 128], fld[f, k]
            )

    spans = windows(levels)
    pk[...] = pack([x[c, own, :] for c in range(channels)], spans, lane_o)
    halo_send_all(*xargs)
    halo_wait_recv(*xargs)
    merged = jnp.where(right_part(spans, lane), pkr[...], pkl[...])
    for c in range(channels):
        hx[c] = unpack(merged, spans[c], lane)

    rows_ok = ((row_e >= TOP) | (a > 0)) & ((row_e < TOP + 128) | (a < n_lat - 1))
    lanes_ok = ((lane >= 64) | (b < n_lon - 1)) & ((lane < 64) | (b > 0))
    halo_ok = rows_ok & lanes_ok
    first, last = lane == 0, lane == 127

    def sides(body, rim):
        ra, rh = pltpu.roll(body, 127, 1), pltpu.roll(rim, 127, 1)
        la, lh = pltpu.roll(body, 1, 1), pltpu.roll(rim, 1, 1)
        return (
            jnp.where(last, rh, ra), jnp.where(first, lh, la),
            jnp.where(last, ra, rh), jnp.where(first, la, lh),
        )

    def next_row(v):
        return pltpu.roll(v, rows_ext - 1, 0)

    def prev_row(v):
        return pltpu.roll(v, 1, 0)

    def levels_sum(ref, base, k, index=slice(None)):
        total = None
        for d in (-1, 1):
            if 0 <= k + d < levels:
                v = ref[base + k + d, index, :]
                total = v if total is None else total + v
        return total

    def levels_diff(ref, base, k, index=slice(None)):
        up = ref[base + k + 1, index, :] if k + 1 < levels else 0.0
        down = ref[base + k - 1, index, :] if k > 0 else 0.0
        return up - down

    gain = gain_s[...]
    for f in range(3):
        for k in range(levels):
            c = f * levels + k
            body, rim = x[c], hx[c]
            r, l, rr, ll = sides(body, rim)
            mid = 4.0 + 2.0 * gain
            lap = next_row(body) + prev_row(body) + gain * (r + l) - mid * body
            lap = lap + levels_sum(x, f * levels, k)
            new = body + va[k] * lap
            lap_h = next_row(rim) + prev_row(rim) + gain * (rr + ll) - mid * rim
            lap_h = lap_h + levels_sum(hx, f * levels, k)
            new_h = rim + vh[k] * lap_h
            if f == 0:
                new = new + BUOYANCY * x[3 * levels + k]
                new_h = new_h + BUOYANCY * hx[3 * levels + k]
            st[c] = jnp.where(rows_ok, new, 0.0)
            sth[c] = jnp.where(halo_ok, new_h, 0.0)

    scale = -0.5 / (4.0 + 2.0 * gain)
    for k in range(levels):
        r, l, rr, ll = sides(st[2 * levels + k], sth[2 * levels + k])
        b1, h1 = st[levels + k], sth[levels + k]
        d = next_row(b1) - prev_row(b1) + inv_s[...] * (r - l) + levels_diff(st, 0, k)
        dh = next_row(h1) - prev_row(h1) + inv_s[...] * (rr - ll) + levels_diff(sth, 0, k)
        p1[k] = jnp.where(rows_ok, scale * d, 0.0)
        p1h[k] = jnp.where(halo_ok, scale * dh, 0.0)

    place = sub8 * 128 + lane8
    tile = jnp.zeros((8, 128), F32)
    for k in range(levels):
        part = coef_a[...] * p1[k] + coef_h[...] * p1h[k]
        part = part + jnp.where(is_own, levels_sum(p1, 0, k), 0.0)
        total = jnp.sum(jnp.sum(part, axis=0, keepdims=True), axis=1, keepdims=True)
        tile = tile + jnp.where(place == me * levels + k, total * (1.0 / 128.0), 0.0)
    mine[...] = tile

    def sum_copy(t, there, i):
        return pltpu.make_async_remote_copy(
            src_ref=mine, dst_ref=sums.at[there],
            send_sem=sum_send.at[i], recv_sem=sum_recv.at[there],
            device_id=dev(p, t // n_lon, lax.rem(t, n_lon)), device_id_type=MESH,
        )

    def send_sum(i, carry):
        sum_copy(lax.rem(me + i, ndev), me, i).start()
        return carry

    lax.fori_loop(1, ndev, send_sum, 0)

    gain_o = gain_s[own, :]
    inv_o = inv_s[own, :]
    first_o, last_o = lane_o == 0, lane_o == 127

    def sides_own(body, rim):
        r = jnp.where(last_o, pltpu.roll(rim, 127, 1), pltpu.roll(body, 127, 1))
        l = jnp.where(first_o, pltpu.roll(rim, 1, 1), pltpu.roll(body, 1, 1))
        return r, l

    for f in range(3, 6):
        for k in range(levels):
            c = f * levels + k
            body = x[c]
            mid = body[TOP : TOP + 128]
            r, l = sides_own(mid, hx[c, own, :])
            lap = next_row(body)[TOP : TOP + 128] + prev_row(body)[TOP : TOP + 128]
            lap = lap + gain_o * (r + l) - (4.0 + 2.0 * gain_o) * mid
            lap = lap + levels_sum(x, f * levels, k, own)
            onew[f, k] = mid + va[k, own, :] * lap
    store_late = pltpu.make_async_copy(
        onew.at[pl.ds(3, 3)], out_ref.at[0, pl.ds(3, 3)], out_sem.at[0]
    )
    store_late.start()
    for k in range(levels):
        body = p1[k]
        mid = body[TOP : TOP + 128]
        r, l = sides_own(mid, p1h[k, own, :])
        diff = next_row(body)[TOP : TOP + 128] - prev_row(body)[TOP : TOP + 128]
        onew[0, k] = st[k, own, :] - 0.5 * levels_diff(p1, 0, k, own)
        onew[1, k] = st[levels + k, own, :] - 0.5 * diff
        onew[2, k] = st[2 * levels + k, own, :] - 0.5 * inv_o * (r - l)

    for c in load_o:
        c.wait()

    def take_sum(i, total):
        s = lax.rem(me + i, ndev)
        sum_copy(me, s, 0).wait_recv()
        return total + sums[s]

    vec = lax.fori_loop(1, ndev, take_sum, mine[...])

    def coarse(t, k):
        prod = opr[t, k] * vec
        return jnp.sum(jnp.sum(prod, axis=0, keepdims=True), axis=1, keepdims=True)

    zero = jnp.zeros((1, 1), F32)
    mid_c = [coarse(0, k) for k in range(levels)]
    row_o = lax.broadcasted_iota(jnp.int32, (128, 128), 0)
    for k in range(levels):
        up = jnp.where(a > 0, coarse(1, k), zero)
        down = jnp.where(a < n_lat - 1, coarse(2, k), zero)
        west = jnp.where(b > 0, coarse(3, k), zero)
        east = jnp.where(b < n_lon - 1, coarse(4, k), zero)
        c = mid_c[k]
        opress[k] = p1[k, own, :] + c
        high = mid_c[k + 1] if k + 1 < levels else zero
        low = mid_c[k - 1] if k > 0 else zero
        onew[0, k] = onew[0, k] - 0.5 * (high - low)
        fix = jnp.where(row_o == 0, c - up, 0.0) + jnp.where(row_o == 127, down - c, 0.0)
        onew[1, k] = onew[1, k] - 0.5 * fix
        fix = jnp.where(first_o, c - west, 0.0) + jnp.where(last_o, east - c, 0.0)
        onew[2, k] = onew[2, k] - 0.5 * inv_o * fix
    store_new = pltpu.make_async_copy(
        onew.at[pl.ds(0, 3)], out_ref.at[0, pl.ds(0, 3)], out_sem.at[1]
    )
    store_p = pltpu.make_async_copy(opress, press_ref.at[0], out_sem.at[2])
    store_new.start()
    store_p.start()

    def end_lon(q, carry):
        ask_copy(q, b).wait_send()
        rep_copy(q, b).wait_send()
        return carry

    lax.fori_loop(0, n_lon, end_lon, 0)
    halo_wait_send(*vargs)
    halo_wait_send(*xargs)

    def end_sum(i, carry):
        sum_copy(me, me, i).wait_send()
        return carry

    lax.fori_loop(1, ndev, end_sum, 0)
    store_late.wait()
    store_new.wait()
    store_p.wait()


def solution(mesh):
    n_lat, n_lon = mesh.shape["lat"], mesh.shape["lon"]

    def shards(fields, viscosity, partner, src_row, src_col, weight_id, border_angle, dest_cell):
        levels = fields.shape[2]
        blocks = partner.shape[2]
        channels = 6 * levels
        ext = 128 + 2 * TOP
        ndev = n_lat * n_lon
        cells = src_row.shape[2]
        oper = jnp.asarray(coarse_operator(levels, n_lat, n_lon))
        vm = pl.BlockSpec(memory_space=pltpu.VMEM)
        anyw = pl.BlockSpec(memory_space=pl.ANY)
        v = lambda *s: pltpu.VMEM(s, F32)
        sem = lambda n: pltpu.SemaphoreType.DMA((n,))
        return pl.pallas_call(
            functools.partial(kernel, (n_lat, n_lon, levels, blocks)),
            out_shape=(
                jax.ShapeDtypeStruct(fields.shape, F32),
                jax.ShapeDtypeStruct(viscosity.shape, F32),
            ),
            in_specs=[vm] * 6 + [anyw] * 3,
            out_specs=(anyw, anyw),
            scratch_shapes=[
                v(6, levels, 128, 128),
                pltpu.VMEM((6, levels * 128, 256), BF16),
                pltpu.VMEM((n_lon, 8, 128), jnp.int32),
                pltpu.VMEM((n_lon, 8, 128), jnp.int32),
                v(n_lon, channels, 128),
                v(n_lon, channels, 128),
                v(channels, ext, 128),
                v(channels, ext, 128),
                v(128, 128), v(ext, 128), v(ext, 128),
                v(levels, ext, 128), v(levels, ext, 128),
                v(128, 128), v(ext, 128), v(ext, 128),
                v(ext, 128), v(ext, 128), v(ext, 128), v(ext, 128),
                v(3 * levels, ext, 128), v(3 * levels, ext, 128),
                v(levels, ext, 128), v(levels, ext, 128),
                v(128, 128),
                pltpu.VMEM((128, cells), BF16),
                pltpu.VMEM((128, 2 * cells), BF16),
                v(5, levels, 8, 128),
                v(ndev, 8, 128),
                v(8, 128),
                v(6, levels, 128, 128),
                v(levels, 128, 128),
                sem(2), sem(5), sem(3),
                sem(n_lon), sem(n_lon), sem(n_lon), sem(n_lon),
                sem(8), sem(8), sem(8), sem(8), sem(ndev), sem(ndev),
            ],
            compiler_params=pltpu.CompilerParams(
                collective_id=0, has_side_effects=True, vmem_limit_bytes=48 * 1024 * 1024
            ),
            name="shell_step",
        )(
            partner, src_row, src_col, weight_id, border_angle, dest_cell,
            fields, viscosity, oper,
        )

    return jax.shard_map(
        shards,
        mesh=mesh,
        in_specs=(
            P("panel", None, None, "lat", "lon"),
            P("panel", None, "lat", "lon"),
            P("panel", "lat", "lon", None),
            P("panel", "lat", "lon"),
            P("panel", "lat", "lon"),
            P("panel", "lat", "lon"),
            P("panel", "lat", "lon"),
            P("panel", "lat", "lon"),
        ),
        out_specs=(P("panel", None, None, "lat", "lon"), P("panel", None, "lat", "lon")),
        check_vma=False,
    )
```

```python
import functools
import math

import jax
import jax.numpy as jnp
import numpy as np
from jax import lax
from jax.experimental import pallas as pl
from jax.experimental.pallas import tpu as pltpu
from jax.sharding import PartitionSpec as P

MESH = pl.DeviceIdType.MESH
WQ = 8
BUOYANCY = 0.5
TOP = 8
F32 = jnp.float32
BF16 = jnp.bfloat16


def coarse_operator(levels, n_lat, n_lon):
    def table(n):
        m = np.arange(n, dtype=np.float64)
        norm = np.sqrt(np.where(m > 0, 2.0, 1.0) / n)
        q = norm[:, None] * np.cos(np.pi * m[:, None] * (m[None, :] + 0.5) / n)
        return q, 4.0 * np.sin(np.pi * m / (2.0 * n)) ** 2

    qr, er = table(levels)
    qa, ea = table(n_lat)
    qo, eo = table(n_lon)
    inv = 1.0 / (
        ea[:, None, None] + eo[None, :, None] + er[None, None, :] + 1.0 / (n_lat * n_lon)
    )
    q = np.einsum("ax,oy,rz->aorxyz", qa, qo, qr).reshape(inv.size, inv.size)
    full = (q.T * inv.reshape(-1)) @ q / math.sqrt(n_lat * n_lon)
    count = inv.size
    used = -(-count // 128)
    wide = np.zeros((count, used * 128), np.float32)
    wide[:, :count] = full
    return wide.reshape(n_lat * n_lon, levels, used, 128)


GROUPS = ((0, 4), (4, 6))
WIDTHS = (3, 3, 3, 2, 1, 1)


def windows(levels, group):
    spans, at = [], 0
    for width in WIDTHS[group[0] : group[1]]:
        for _ in range(levels):
            spans.append((at + width, width))
            at += 2 * width
    return spans


def visc_windows(levels):
    return [(4 * k + 2, 2) for k in range(levels)]


def pack(tiles, spans, lane):
    packed = None
    for tile, (centre, width) in zip(tiles, spans):
        moved = pltpu.roll(tile, centre, 1)
        inside = (lane >= centre - width) & (lane < centre + width)
        packed = jnp.where(inside, moved, 0.0 if packed is None else packed)
    return packed


def right_part(spans, lane):
    mask = jnp.zeros(lane.shape, jnp.int32)
    for centre, width in spans:
        mask = jnp.where((lane >= centre) & (lane < centre + width), 1, mask)
    return mask > 0


def unpack(merged, span, lane):
    centre, width = span
    moved = pltpu.roll(merged, (128 - centre) % 128, 1)
    return jnp.where((lane < width) | (lane >= 128 - width), moved, 0.0)


def kernel(
    dims,
    partner_in, row_in, col_in, wid_in, ang_in, dest_in, fields_ref, visc_ref, oper_ref,
    out_ref, press_ref,
    partner_ref, row_ref, col_ref, wid_ref, ang_ref, dest_ref,
    fld, fcat, ask, asked, reply0, answer0, reply1, answer1, x, hx,
    pk, pkl, pkr, pk2, pkl2, pkr2, to_up, to_dn, from_up, from_dn,
    to_up2, to_dn2, from_up2, from_dn2, va, vh, vpk, vpl, vpr,
    inv_s, gain_s, coef_a, coef_h, st, sth, p1, p1h, hit_s, rmask, cmask,
    opr, sums, mine, onew, opress,
    in_sem, op_sem, out_sem, ask_send, ask_recv, rep_send, rep_recv,
    halo_send, halo_recv, halo2_send, halo2_recv, v_send, v_recv, sum_send, sum_recv,
):
    n_lat, n_lon, levels, blocks = dims
    ndev = n_lat * n_lon
    channels = 6 * levels
    rows_ext = 128 + 2 * TOP
    pairs = blocks // 2
    cells = blocks * 64
    p = lax.axis_index("panel")
    a = lax.axis_index("lat")
    b = lax.axis_index("lon")
    me = a * n_lon + b
    own = pl.ds(TOP, 128)

    def dev(panel, lat, lon):
        return {"panel": panel, "lat": lat, "lon": lon}

    load_f = pltpu.make_async_copy(fields_ref.at[0], fld, in_sem.at[0])
    load_v = pltpu.make_async_copy(visc_ref.at[0], va.at[:, own, :], in_sem.at[1])
    small = [
        pltpu.make_async_copy(src, dst, in_sem.at[2 + i])
        for i, (src, dst) in enumerate(
            (
                (partner_in, partner_ref), (row_in, row_ref), (col_in, col_ref),
                (wid_in, wid_ref), (ang_in, ang_ref), (dest_in, dest_ref),
            )
        )
    ]
    for c in small:
        c.start()
    load_f.start()
    load_v.start()
    targets = (
        me,
        jnp.maximum(a - 1, 0) * n_lon + b,
        jnp.minimum(a + 1, n_lat - 1) * n_lon + b,
        a * n_lon + jnp.maximum(b - 1, 0),
        a * n_lon + jnp.minimum(b + 1, n_lon - 1),
    )
    load_o = [
        pltpu.make_async_copy(oper_ref.at[t], opr.at[i], op_sem.at[i])
        for i, t in enumerate(targets)
    ]
    for c in load_o:
        c.start()

    barrier = pltpu.get_barrier_semaphore()

    def greet(i, carry):
        t = lax.rem(me + i, ndev)
        pl.semaphore_signal(
            barrier, inc=1, device_id=dev(p, t // n_lon, lax.rem(t, n_lon)), device_id_type=MESH
        )
        return carry

    lax.fori_loop(1, ndev, greet, 0)

    def greet_other(i, carry):
        pl.semaphore_signal(barrier, inc=1, device_id=dev(1 - p, a, i), device_id_type=MESH)
        return carry

    lax.fori_loop(0, n_lon, greet_other, 0)

    lane8 = lax.broadcasted_iota(jnp.int32, (8, 128), 1)
    sub8 = lax.broadcasted_iota(jnp.int32, (8, 128), 0)
    half = lane8 // 64
    zero_rows = jnp.zeros((6 * levels, TOP, 128), F32)
    x[:, 0:TOP, :] = zero_rows
    x[:, TOP + 128 : rows_ext, :] = zero_rows
    for c in small[:4]:
        c.wait()
    named = jnp.broadcast_to(partner_ref[0], (blocks, blocks)).astype(F32)
    diag = lax.broadcasted_iota(jnp.int32, (blocks, blocks), 0) == lax.broadcasted_iota(
        jnp.int32, (blocks, blocks), 1
    )
    pv = jnp.sum(jnp.where(diag, named, 0.0), axis=1, keepdims=True).astype(jnp.int32)
    pv = jnp.broadcast_to(pv, (blocks, 128))
    block_id = lax.broadcasted_iota(jnp.int32, (blocks, 128), 0)
    before = jnp.zeros((blocks, 128), jnp.int32)
    for k in range(blocks):
        before = before + jnp.where((pv == pv[k : k + 1]) & (block_id > k), 1, 0)
    slot = pv * 2 + before
    keys, keys_r, tiles, tiles_r = [], [], [], []
    for j in range(pairs):
        s0 = jnp.broadcast_to(slot[2 * j : 2 * j + 1], (8, 128))
        s1 = jnp.broadcast_to(slot[2 * j + 1 : 2 * j + 2], (8, 128))
        key = jnp.where(half == 0, s0, s1)
        at = pl.ds(128 * j, 128)
        rr = jnp.broadcast_to(row_ref[0, :, at], (8, 128))
        cc = jnp.broadcast_to(col_ref[0, :, at], (8, 128))
        ww = jnp.broadcast_to(wid_ref[0, :, at], (8, 128))
        tile = jnp.where(sub8 == 0, rr, jnp.where(sub8 == 1, cc, ww))
        keys.append(key)
        tiles.append(tile)
        keys_r.append(pltpu.roll(key, 64, 1))
        tiles_r.append(pltpu.roll(tile, 64, 1))
    for q in range(n_lon):
        want = 2 * q + half
        acc = jnp.zeros((8, 128), jnp.int32)
        for j in range(pairs):
            acc = jnp.where(keys[j] == want, tiles[j], acc)
            acc = jnp.where(keys_r[j] == want, tiles_r[j], acc)
        ask[q] = acc[0:4]

    pl.semaphore_wait(barrier, ndev - 1 + n_lon)

    def ask_copy(q, there):
        return pltpu.make_async_remote_copy(
            src_ref=ask.at[q], dst_ref=asked.at[there],
            send_sem=ask_send.at[q], recv_sem=ask_recv.at[there],
            device_id=dev(1 - p, a, q), device_id_type=MESH,
        )

    def send_ask(i, carry):
        q = lax.rem(b + i, n_lon)
        ask_copy(q, b).start()
        return carry

    lax.fori_loop(0, n_lon, send_ask, 0)

    ways = [(da, db) for da in (-1, 0, 1) for db in (-1, 0, 1) if (da, db) != (0, 0)]

    def exists(da, db):
        ok = None
        for pos, d, n in ((a, da, n_lat), (b, db, n_lon)):
            if d:
                c = (pos > 0) if d < 0 else (pos < n - 1)
                ok = c if ok is None else jnp.logical_and(ok, c)
        return ok

    def halo_copy(w, h):
        da, db = ways[w]
        src_rows = {-1: pl.ds(0, TOP), 0: pl.ds(0, 128), 1: pl.ds(128 - TOP, TOP)}[da]
        dst_rows = {-1: pl.ds(TOP + 128, TOP), 0: own, 1: pl.ds(0, TOP)}[da]
        if db == 0 and h["rows"] is not None:
            up, dn, got_up, got_dn = h["rows"]
            src, dst = (up, got_dn) if da < 0 else (dn, got_up)
        elif db == 0:
            src = h["body"].at[:, pl.ds(TOP if da < 0 else 128, TOP), :]
            dst = h["body"].at[:, dst_rows, :]
        else:
            into = h["cols"][1 if db > 0 else 2]
            src = h["cols"][0].at[src_rows, :]
            dst = into if h["flat"] else into.at[dst_rows, :]
        return pltpu.make_async_remote_copy(
            src_ref=src, dst_ref=dst, send_sem=h["send"].at[w], recv_sem=h["recv"].at[w],
            device_id=dev(p, a + da, b + db), device_id_type=MESH,
        )

    def ways_of(h):
        return [w for w, (da, db) in enumerate(ways) if not (h["flat"] and da and db)]

    def halo_send_all(h):
        for w in ways_of(h):
            @pl.when(exists(*ways[w]))
            def _(w=w):
                halo_copy(w, h).start()

    def halo_wait_recv(h):
        for w in ways_of(h):
            da, db = ways[w]

            @pl.when(exists(-da, -db))
            def _(w=w):
                halo_copy(w, h).wait_recv()

    def halo_wait_send(h):
        for w in ways_of(h):
            @pl.when(exists(*ways[w]))
            def _(w=w):
                halo_copy(w, h).wait_send()

    def halo_clear(h):
        for w in ways_of(h):
            da, db = ways[w]
            dst_rows = {-1: pl.ds(TOP + 128, TOP), 0: own, 1: pl.ds(0, TOP)}[da]
            if db == 0 and h["rows"] is not None:
                continue

            @pl.when(jnp.logical_not(exists(-da, -db)))
            def _(da=da, db=db, dst_rows=dst_rows):
                if db == 0:
                    h["body"][:, dst_rows, :] = jnp.zeros((levels, TOP, 128), F32)
                else:
                    buf = h["cols"][1 if db > 0 else 2]
                    if h["flat"]:
                        buf[...] = jnp.zeros((128, 128), F32)
                    else:
                        buf[dst_rows, :] = jnp.zeros((128 if da == 0 else TOP, 128), F32)

    def rows_of(group):
        spots, at = [], 0
        for f in range(*group):
            for k in range(levels):
                spots.append((f * levels + k, at, WIDTHS[f]))
                at += WIDTHS[f]
        return spots

    def pack_rows(group, h):
        up, dn = h["rows"][0:2]

        @pl.when(a > 0)
        def _():
            for c, at, w in rows_of(group):
                up[at : at + w, :] = x[c, TOP : TOP + w, :]

        @pl.when(a < n_lat - 1)
        def _():
            for c, at, w in rows_of(group):
                dn[at : at + w, :] = x[c, TOP + 128 - w : TOP + 128, :]

    def unpack_rows(group, h):
        got_up, got_dn = h["rows"][2:4]

        @pl.when(a > 0)
        def _():
            for c, at, w in rows_of(group):
                x[c, TOP - w : TOP, :] = got_up[at : at + w, :]

        @pl.when(a < n_lat - 1)
        def _():
            for c, at, w in rows_of(group):
                x[c, TOP + 128 : TOP + 128 + w, :] = got_dn[at : at + w, :]

    lane = lax.broadcasted_iota(jnp.int32, (rows_ext, 128), 1)
    lane_o = lax.broadcasted_iota(jnp.int32, (128, 128), 1)
    row_e = lax.broadcasted_iota(jnp.int32, (rows_ext, 128), 0)

    vargs = dict(
        rows=None, body=va, cols=(vpk, vpl, vpr), flat=False, send=v_send, recv=v_recv
    )
    hargs = (
        dict(
            rows=(to_up, to_dn, from_up, from_dn), cols=(pk, pkl, pkr), flat=False,
            send=halo_send, recv=halo_recv,
        ),
        dict(
            rows=(to_up2, to_dn2, from_up2, from_dn2), cols=(pk2, pkl2, pkr2), flat=True,
            send=halo2_send, recv=halo2_recv,
        ),
    )
    halo_clear(vargs)
    load_v.wait()
    vpk[...] = pack([va[k, own, :] for k in range(levels)], visc_windows(levels), lane_o)
    halo_send_all(vargs)
    halo_clear(hargs[0])
    halo_clear(hargs[1])

    load_f.wait()
    for f in range(6):
        v = fld[f].reshape(levels * 128, 128)
        hi = v.astype(BF16)
        lo = (v - hi.astype(F32)).astype(BF16)
        fcat[f, :, 0:128] = hi
        fcat[f, :, 128:256] = lo

    small[4].wait()
    cos_a = jnp.cos(ang_ref[0])
    sin_a = jnp.sin(ang_ref[0])
    colat = math.pi / 4.0 + ((a * 128 + row_e - TOP).astype(F32) + 0.5) * (
        math.pi / 2.0
    ) / (n_lat * 128)
    inv = 1.0 / jnp.sin(colat)
    gain = inv * inv
    inv_s[...] = inv
    gain_s[...] = gain
    is_own = (row_e >= TOP) & (row_e < TOP + 128)
    edge_lane = (lane == 0) | (lane == 127)
    ca = 2.0 + 2.0 * gain
    ca = ca - jnp.where((row_e == TOP) | (row_e == TOP + 127), 1.0, 0.0)
    ca = ca - jnp.where(edge_lane, gain, 0.0)
    rim = jnp.where((row_e == TOP - 1) | (row_e == TOP + 128), 1.0, 0.0)
    coef_a[...] = jnp.where(is_own, ca, rim)
    coef_h[...] = jnp.where(is_own & edge_lane, gain, 0.0)

    replies, answers = (reply0, reply1), (answer0, answer1)

    def rep_copy(g, q, there):
        return pltpu.make_async_remote_copy(
            src_ref=replies[g].at[q], dst_ref=answers[g].at[there],
            send_sem=rep_send.at[g * n_lon + q], recv_sem=rep_recv.at[g * n_lon + there],
            device_id=dev(1 - p, a, q), device_id_type=MESH,
        )

    sub_c = lax.broadcasted_iota(jnp.int32, (128, 256), 0)

    def serve(g, i, carry):
        pr = lax.rem(b // 2 + i, n_lon // 2)
        q0 = 2 * pr
        if g == 0:
            ask_copy(0, q0).wait_recv()
            ask_copy(0, q0 + 1).wait_recv()
        r0 = asked[q0]
        r1 = asked[q0 + 1]
        rr = jnp.concatenate([r0[0:1], r1[0:1]], axis=1)
        cc = jnp.concatenate([r0[1:2], r1[1:2]], axis=1)
        ww = jnp.concatenate([r0[2:3], r1[2:3]], axis=1)
        fa = ((ww >> 3).astype(F32) + 0.5) / WQ
        fo = ((ww & 7).astype(F32) + 0.5) / WQ
        cw = jnp.where(sub_c == cc, 1.0 - fo, jnp.where(sub_c == cc + 1, fo, 0.0)).astype(BF16)
        rw = jnp.where(sub_c == rr, 1.0 - fa, jnp.where(sub_c == rr + 1, fa, 0.0))
        cw2 = jnp.concatenate([cw, cw], axis=0)
        parts = []
        for f in range(*GROUPS[g]):
            v = jnp.dot(fcat[f], cw2, preferred_element_type=F32)
            parts.append(jnp.sum(v.reshape(levels, 128, 256) * rw[None], axis=1))
        res = jnp.concatenate(parts, axis=0)
        replies[g][q0] = res[:, 0:128]
        replies[g][q0 + 1] = res[:, 128:256]
        rep_copy(g, q0, b).start()
        rep_copy(g, q0 + 1, b).start()
        return carry

    lax.fori_loop(0, n_lon // 2, functools.partial(serve, 0), 0)
    small[5].wait()
    dest = dest_ref[0]
    sub_d = lax.broadcasted_iota(jnp.int32, (128, cells), 0)
    rm = jnp.where(sub_d == dest // 128, 1.0, 0.0).astype(BF16)
    cm = jnp.where(sub_d == dest % 128, 1.0, 0.0).astype(BF16)
    rmask[...] = rm
    cmask[:, 0:cells] = cm
    cmask[:, cells : 2 * cells] = cm
    nt = (((1,), (1,)), ((), ()))
    hit_s[...] = lax.dot_general(rm, cm, nt, preferred_element_type=F32)
    lax.fori_loop(0, n_lon // 2, functools.partial(serve, 1), 0)
    halo_wait_recv(vargs)
    vmerged = jnp.where(right_part(visc_windows(levels), lane), vpr[...], vpl[...])
    for k in range(levels):
        vh[k] = unpack(vmerged, visc_windows(levels)[k], lane)

    half_row = half[0:1]

    def fill(g):
        first_f, end_f = GROUPS[g]

        def wait_rep(q, carry):
            rep_copy(g, 0, q).wait_recv()
            return carry

        lax.fori_loop(0, n_lon, wait_rep, 0)
        got = [answers[g][q] for q in range(n_lon)]
        got_r = [pltpu.roll(v, 64, 1) for v in got]
        picked = []
        for j in range(pairs):
            key = keys[j][0:1]
            acc = jnp.zeros(((end_f - first_f) * levels, 128), F32)
            for q in range(n_lon):
                acc = jnp.where(key == 2 * q + half_row, got[q], acc)
                acc = jnp.where(key == 2 * q + 1 - half_row, got_r[q], acc)
            picked.append(acc)
        values = jnp.concatenate(picked, axis=1)
        fv = [values[f * levels : (f + 1) * levels] for f in range(end_f - first_f)]
        if g == 0:
            turned = [
                fv[0], cos_a * fv[1] + sin_a * fv[2], cos_a * fv[2] - sin_a * fv[1], fv[3],
            ]
        else:
            turned = [cos_a * fv[0] + sin_a * fv[1], cos_a * fv[1] - sin_a * fv[0]]
        hit = hit_s[...] > 0.5
        for f in range(first_f, end_f):
            v = turned[f - first_f]
            hi = v.astype(BF16)
            lo = (v - hi.astype(F32)).astype(BF16)
            left = []
            for k in range(levels):
                left.append(
                    jnp.concatenate(
                        [rmask[...] * hi[k : k + 1], rmask[...] * lo[k : k + 1]], axis=1
                    )
                )
            put = lax.dot_general(
                jnp.concatenate(left, axis=0), cmask[...], nt, preferred_element_type=F32
            )
            for k in range(levels):
                x[f * levels + k, own, :] = jnp.where(
                    hit, put[k * 128 : (k + 1) * 128], fld[f, k]
                )
        h = hargs[g]
        pack_rows(GROUPS[g], h)
        h["cols"][0][...] = pack(
            [x[c, own, :] for c in range(first_f * levels, end_f * levels)],
            windows(levels, GROUPS[g]), lane_o,
        )
        halo_send_all(h)

    fill(0)
    fill(1)
    halo_wait_recv(hargs[0])
    unpack_rows(GROUPS[0], hargs[0])
    spans = windows(levels, GROUPS[0])
    merged = jnp.where(right_part(spans, lane), pkr[...], pkl[...])
    for c, span in enumerate(spans):
        hx[c] = unpack(merged, span, lane)

    rows_ok = ((row_e >= TOP) | (a > 0)) & ((row_e < TOP + 128) | (a < n_lat - 1))
    lanes_ok = ((lane >= 64) | (b < n_lon - 1)) & ((lane < 64) | (b > 0))
    halo_ok = rows_ok & lanes_ok
    first, last = lane == 0, lane == 127

    def sides(body, rim):
        ra, rh = pltpu.roll(body, 127, 1), pltpu.roll(rim, 127, 1)
        la, lh = pltpu.roll(body, 1, 1), pltpu.roll(rim, 1, 1)
        return (
            jnp.where(last, rh, ra), jnp.where(first, lh, la),
            jnp.where(last, ra, rh), jnp.where(first, la, lh),
        )

    def next_row(v):
        return pltpu.roll(v, rows_ext - 1, 0)

    def prev_row(v):
        return pltpu.roll(v, 1, 0)

    def levels_sum(ref, base, k, index=slice(None)):
        total = None
        for d in (-1, 1):
            if 0 <= k + d < levels:
                v = ref[base + k + d, index, :]
                total = v if total is None else total + v
        return total

    def levels_diff(ref, base, k, index=slice(None)):
        up = ref[base + k + 1, index, :] if k + 1 < levels else 0.0
        down = ref[base + k - 1, index, :] if k > 0 else 0.0
        return up - down

    gain = gain_s[...]
    for f in range(3):
        for k in range(levels):
            c = f * levels + k
            body, rim = x[c], hx[c]
            r, l, rr, ll = sides(body, rim)
            mid = 4.0 + 2.0 * gain
            lap = next_row(body) + prev_row(body) + gain * (r + l) - mid * body
            lap = lap + levels_sum(x, f * levels, k)
            new = body + va[k] * lap
            lap_h = next_row(rim) + prev_row(rim) + gain * (rr + ll) - mid * rim
            lap_h = lap_h + levels_sum(hx, f * levels, k)
            new_h = rim + vh[k] * lap_h
            if f == 0:
                new = new + BUOYANCY * x[3 * levels + k]
                new_h = new_h + BUOYANCY * hx[3 * levels + k]
            st[c] = jnp.where(rows_ok, new, 0.0)
            sth[c] = jnp.where(halo_ok, new_h, 0.0)

    scale = -0.5 / (4.0 + 2.0 * gain)
    for k in range(levels):
        r, l, rr, ll = sides(st[2 * levels + k], sth[2 * levels + k])
        b1, h1 = st[levels + k], sth[levels + k]
        d = next_row(b1) - prev_row(b1) + inv_s[...] * (r - l) + levels_diff(st, 0, k)
        dh = next_row(h1) - prev_row(h1) + inv_s[...] * (rr - ll) + levels_diff(sth, 0, k)
        p1[k] = jnp.where(rows_ok, scale * d, 0.0)
        p1h[k] = jnp.where(halo_ok, scale * dh, 0.0)

    shape = mine.shape
    place = lax.broadcasted_iota(jnp.int32, shape, 0) * 128
    place = place + lax.broadcasted_iota(jnp.int32, shape, 1)
    tile = jnp.zeros(shape, F32)
    for k in range(levels):
        part = coef_a[...] * p1[k] + coef_h[...] * p1h[k]
        part = part + jnp.where(is_own, levels_sum(p1, 0, k), 0.0)
        total = jnp.sum(jnp.sum(part, axis=0, keepdims=True), axis=1, keepdims=True)
        tile = tile + jnp.where(place == me * levels + k, total * (1.0 / 128.0), 0.0)
    mine[...] = tile

    def sum_copy(t, there, i):
        return pltpu.make_async_remote_copy(
            src_ref=mine, dst_ref=sums.at[there],
            send_sem=sum_send.at[i], recv_sem=sum_recv.at[there],
            device_id=dev(p, t // n_lon, lax.rem(t, n_lon)), device_id_type=MESH,
        )

    def send_sum(i, carry):
        sum_copy(lax.rem(me + i, ndev), me, i).start()
        return carry

    lax.fori_loop(1, ndev, send_sum, 0)

    gain_o = gain_s[own, :]
    inv_o = inv_s[own, :]
    first_o, last_o = lane_o == 0, lane_o == 127

    def sides_own(body, rim):
        r = jnp.where(last_o, pltpu.roll(rim, 127, 1), pltpu.roll(body, 127, 1))
        l = jnp.where(first_o, pltpu.roll(rim, 1, 1), pltpu.roll(body, 1, 1))
        return r, l

    halo_wait_recv(hargs[1])
    unpack_rows(GROUPS[1], hargs[1])
    spans = windows(levels, GROUPS[1])
    merged = jnp.where(right_part(spans, lane_o), pkr2[...], pkl2[...])
    for c, span in enumerate(spans):
        hx[4 * levels + c, own, :] = unpack(merged, span, lane_o)
    for f in range(3, 6):
        for k in range(levels):
            c = f * levels + k
            body = x[c]
            mid = body[TOP : TOP + 128]
            r, l = sides_own(mid, hx[c, own, :])
            lap = next_row(body)[TOP : TOP + 128] + prev_row(body)[TOP : TOP + 128]
            lap = lap + gain_o * (r + l) - (4.0 + 2.0 * gain_o) * mid
            lap = lap + levels_sum(x, f * levels, k, own)
            onew[f, k] = mid + va[k, own, :] * lap
    store_late = pltpu.make_async_copy(
        onew.at[pl.ds(3, 3)], out_ref.at[0, pl.ds(3, 3)], out_sem.at[0]
    )
    store_late.start()
    for k in range(levels):
        body = p1[k]
        mid = body[TOP : TOP + 128]
        r, l = sides_own(mid, p1h[k, own, :])
        diff = next_row(body)[TOP : TOP + 128] - prev_row(body)[TOP : TOP + 128]
        onew[0, k] = st[k, own, :] - 0.5 * levels_diff(p1, 0, k, own)
        onew[1, k] = st[levels + k, own, :] - 0.5 * diff
        onew[2, k] = st[2 * levels + k, own, :] - 0.5 * inv_o * (r - l)

    for c in load_o:
        c.wait()

    def take_sum(i, total):
        s = lax.rem(me + i, ndev)
        sum_copy(me, s, 0).wait_recv()
        return total + sums[s]

    vec = lax.fori_loop(1, ndev, take_sum, mine[...])

    def coarse(t, k):
        prod = opr[t, k] * vec
        return jnp.sum(jnp.sum(prod, axis=0, keepdims=True), axis=1, keepdims=True)

    zero = jnp.zeros((1, 1), F32)
    mid_c = [coarse(0, k) for k in range(levels)]
    row_o = lax.broadcasted_iota(jnp.int32, (128, 128), 0)
    for k in range(levels):
        up = jnp.where(a > 0, coarse(1, k), zero)
        down = jnp.where(a < n_lat - 1, coarse(2, k), zero)
        west = jnp.where(b > 0, coarse(3, k), zero)
        east = jnp.where(b < n_lon - 1, coarse(4, k), zero)
        c = mid_c[k]
        opress[k] = p1[k, own, :] + c
        high = mid_c[k + 1] if k + 1 < levels else zero
        low = mid_c[k - 1] if k > 0 else zero
        onew[0, k] = onew[0, k] - 0.5 * (high - low)
        fix = jnp.where(row_o == 0, c - up, 0.0) + jnp.where(row_o == 127, down - c, 0.0)
        onew[1, k] = onew[1, k] - 0.5 * fix
        fix = jnp.where(first_o, c - west, 0.0) + jnp.where(last_o, east - c, 0.0)
        onew[2, k] = onew[2, k] - 0.5 * inv_o * fix
    store_new = pltpu.make_async_copy(
        onew.at[pl.ds(0, 3)], out_ref.at[0, pl.ds(0, 3)], out_sem.at[1]
    )
    store_p = pltpu.make_async_copy(opress, press_ref.at[0], out_sem.at[2])
    store_new.start()
    store_p.start()

    def end_lon(q, carry):
        ask_copy(q, b).wait_send()
        rep_copy(0, q, b).wait_send()
        rep_copy(1, q, b).wait_send()
        return carry

    lax.fori_loop(0, n_lon, end_lon, 0)
    halo_wait_send(vargs)
    halo_wait_send(hargs[0])
    halo_wait_send(hargs[1])

    def end_sum(i, carry):
        sum_copy(me, me, i).wait_send()
        return carry

    lax.fori_loop(1, ndev, end_sum, 0)
    store_late.wait()
    store_new.wait()
    store_p.wait()


def solution(mesh):
    n_lat, n_lon = mesh.shape["lat"], mesh.shape["lon"]

    def shards(fields, viscosity, partner, src_row, src_col, weight_id, border_angle, dest_cell):
        levels = fields.shape[2]
        blocks = partner.shape[2]
        channels = 6 * levels
        ext = 128 + 2 * TOP
        ndev = n_lat * n_lon
        cells = src_row.shape[2]
        oper = jnp.asarray(coarse_operator(levels, n_lat, n_lon))
        anyw = pl.BlockSpec(memory_space=pl.ANY)
        v = lambda *s: pltpu.VMEM(s, F32)
        vi = lambda *s: pltpu.VMEM(s, jnp.int32)
        sem = lambda n: pltpu.SemaphoreType.DMA((n,))
        rows0, rows1 = 11 * levels, 2 * levels
        used = oper.shape[2]
        return pl.pallas_call(
            functools.partial(kernel, (n_lat, n_lon, levels, blocks)),
            out_shape=(
                jax.ShapeDtypeStruct(fields.shape, F32),
                jax.ShapeDtypeStruct(viscosity.shape, F32),
            ),
            in_specs=[anyw] * 9,
            out_specs=(anyw, anyw),
            scratch_shapes=[
                vi(1, 1, blocks), vi(1, 1, cells), vi(1, 1, cells), vi(1, 1, cells),
                v(1, 1, cells), vi(1, 1, cells),
                v(6, levels, 128, 128),
                pltpu.VMEM((6, levels * 128, 256), BF16),
                vi(n_lon, 4, 128), vi(n_lon, 4, 128),
                v(n_lon, 4 * levels, 128), v(n_lon, 4 * levels, 128),
                v(n_lon, 2 * levels, 128), v(n_lon, 2 * levels, 128),
                v(channels, ext, 128),
                v(channels, ext, 128),
                v(128, 128), v(ext, 128), v(ext, 128),
                v(128, 128), v(128, 128), v(128, 128),
                v(rows0, 128), v(rows0, 128), v(rows0, 128), v(rows0, 128),
                v(rows1, 128), v(rows1, 128), v(rows1, 128), v(rows1, 128),
                v(levels, ext, 128), v(levels, ext, 128),
                v(128, 128), v(ext, 128), v(ext, 128),
                v(ext, 128), v(ext, 128), v(ext, 128), v(ext, 128),
                v(3 * levels, ext, 128), v(3 * levels, ext, 128),
                v(levels, ext, 128), v(levels, ext, 128),
                v(128, 128),
                pltpu.VMEM((128, cells), BF16),
                pltpu.VMEM((128, 2 * cells), BF16),
                v(5, levels, used, 128),
                v(ndev, used, 128),
                v(used, 128),
                v(6, levels, 128, 128),
                v(levels, 128, 128),
                sem(8), sem(5), sem(3),
                sem(n_lon), sem(n_lon), sem(2 * n_lon), sem(2 * n_lon),
                sem(8), sem(8), sem(8), sem(8), sem(8), sem(8), sem(ndev), sem(ndev),
            ],
            compiler_params=pltpu.CompilerParams(
                collective_id=0, has_side_effects=True, vmem_limit_bytes=60 * 1024 * 1024
            ),
            name="shell_step",
        )(
            partner.reshape(1, 1, blocks), src_row, src_col, weight_id, border_angle, dest_cell,
            fields, viscosity, oper,
        )

    return jax.shard_map(
        shards,
        mesh=mesh,
        in_specs=(
            P("panel", None, None, "lat", "lon"),
            P("panel", None, "lat", "lon"),
            P("panel", "lat", "lon", None),
            P("panel", "lat", "lon"),
            P("panel", "lat", "lon"),
            P("panel", "lat", "lon"),
            P("panel", "lat", "lon"),
            P("panel", "lat", "lon"),
        ),
        out_specs=(P("panel", None, None, "lat", "lon"), P("panel", None, "lat", "lon")),
        check_vma=False,
    )
```

```python
import functools
import math

import jax
import jax.numpy as jnp
import numpy as np
from jax import lax
from jax.experimental import pallas as pl
from jax.experimental.pallas import tpu as pltpu
from jax.sharding import PartitionSpec as P

MESH = pl.DeviceIdType.MESH
WQ = 8
BUOYANCY = 0.5
TOP = 8
F32 = jnp.float32
BF16 = jnp.bfloat16


def coarse_operator(levels, n_lat, n_lon):
    def table(n):
        m = np.arange(n, dtype=np.float64)
        norm = np.sqrt(np.where(m > 0, 2.0, 1.0) / n)
        q = norm[:, None] * np.cos(np.pi * m[:, None] * (m[None, :] + 0.5) / n)
        return q, 4.0 * np.sin(np.pi * m / (2.0 * n)) ** 2

    qr, er = table(levels)
    qa, ea = table(n_lat)
    qo, eo = table(n_lon)
    inv = 1.0 / (
        ea[:, None, None] + eo[None, :, None] + er[None, None, :] + 1.0 / (n_lat * n_lon)
    )
    q = np.einsum("ax,oy,rz->aorxyz", qa, qo, qr).reshape(inv.size, inv.size)
    full = (q.T * inv.reshape(-1)) @ q / math.sqrt(n_lat * n_lon)
    count = inv.size
    used = -(-count // 128)
    wide = np.zeros((count, used * 128), np.float32)
    wide[:, :count] = full
    return wide.reshape(n_lat * n_lon, levels, used, 128)


GROUPS = ((0, 4), (4, 6))
WIDTHS = (3, 3, 3, 2, 1, 1)


def windows(levels, group):
    spans, at = [], 0
    for width in WIDTHS[group[0] : group[1]]:
        for _ in range(levels):
            spans.append((at + width, width))
            at += 2 * width
    return spans


def visc_windows(levels):
    return [(4 * k + 2, 2) for k in range(levels)]


def pack(tiles, spans, lane):
    packed = None
    for tile, (centre, width) in zip(tiles, spans):
        moved = pltpu.roll(tile, centre, 1)
        inside = (lane >= centre - width) & (lane < centre + width)
        packed = jnp.where(inside, moved, 0.0 if packed is None else packed)
    return packed


def right_part(spans, lane):
    mask = jnp.zeros(lane.shape, jnp.int32)
    for centre, width in spans:
        mask = jnp.where((lane >= centre) & (lane < centre + width), 1, mask)
    return mask > 0


def unpack(merged, span, lane):
    centre, width = span
    moved = pltpu.roll(merged, (128 - centre) % 128, 1)
    return jnp.where((lane < width) | (lane >= 128 - width), moved, 0.0)


def kernel(
    dims,
    partner_in, row_in, col_in, wid_in, ang_in, dest_in, fields_ref, visc_ref, oper_ref,
    out_ref, press_ref, cv_ref,
    partner_ref, row_ref, col_ref, wid_ref, ang_ref, dest_ref,
    fld, fcat, ask, asked, reply0, answer0, reply1, answer1, x, hx,
    pk, pkl, pkr, pk2, pkl2, pkr2, to_up, to_dn, from_up, from_dn,
    to_up2, to_dn2, from_up2, from_dn2, va, vh, vpk, vpl, vpr,
    inv_s, gain_s, coef_a, coef_h, st, sth, p1, p1h, hit_s, rmask, cmask,
    opr, sums, mine, onew, cvals,
    in_sem, op_sem, out_sem, ask_send, ask_recv, rep_send, rep_recv,
    halo_send, halo_recv, halo2_send, halo2_recv, v_send, v_recv, sum_send, sum_recv,
):
    n_lat, n_lon, levels, blocks = dims
    ndev = n_lat * n_lon
    channels = 6 * levels
    rows_ext = 128 + 2 * TOP
    pairs = blocks // 2
    cells = blocks * 64
    p = lax.axis_index("panel")
    a = lax.axis_index("lat")
    b = lax.axis_index("lon")
    me = a * n_lon + b
    own = pl.ds(TOP, 128)

    def dev(panel, lat, lon):
        return {"panel": panel, "lat": lat, "lon": lon}

    load_f = pltpu.make_async_copy(fields_ref.at[0], fld, in_sem.at[0])
    load_v = pltpu.make_async_copy(visc_ref.at[0], va.at[:, own, :], in_sem.at[1])
    small = [
        pltpu.make_async_copy(src, dst, in_sem.at[2 + i])
        for i, (src, dst) in enumerate(
            (
                (partner_in, partner_ref), (row_in, row_ref), (col_in, col_ref),
                (wid_in, wid_ref), (ang_in, ang_ref), (dest_in, dest_ref),
            )
        )
    ]
    for c in small:
        c.start()
    load_f.start()
    load_v.start()
    targets = (
        me,
        jnp.maximum(a - 1, 0) * n_lon + b,
        jnp.minimum(a + 1, n_lat - 1) * n_lon + b,
        a * n_lon + jnp.maximum(b - 1, 0),
        a * n_lon + jnp.minimum(b + 1, n_lon - 1),
    )
    load_o = [
        pltpu.make_async_copy(oper_ref.at[t], opr.at[i], op_sem.at[i])
        for i, t in enumerate(targets)
    ]
    for c in load_o:
        c.start()

    barrier = pltpu.get_barrier_semaphore()

    def greet(i, carry):
        t = lax.rem(me + i, ndev)
        pl.semaphore_signal(
            barrier, inc=1, device_id=dev(p, t // n_lon, lax.rem(t, n_lon)), device_id_type=MESH
        )
        return carry

    lax.fori_loop(1, ndev, greet, 0)

    def greet_other(i, carry):
        pl.semaphore_signal(barrier, inc=1, device_id=dev(1 - p, a, i), device_id_type=MESH)
        return carry

    lax.fori_loop(0, n_lon, greet_other, 0)

    lane8 = lax.broadcasted_iota(jnp.int32, (8, 128), 1)
    sub8 = lax.broadcasted_iota(jnp.int32, (8, 128), 0)
    half = lane8 // 64
    zero_rows = jnp.zeros((6 * levels, TOP, 128), F32)
    x[:, 0:TOP, :] = zero_rows
    x[:, TOP + 128 : rows_ext, :] = zero_rows
    for c in small[:4]:
        c.wait()
    named = jnp.broadcast_to(partner_ref[0], (blocks, blocks)).astype(F32)
    diag = lax.broadcasted_iota(jnp.int32, (blocks, blocks), 0) == lax.broadcasted_iota(
        jnp.int32, (blocks, blocks), 1
    )
    pv = jnp.sum(jnp.where(diag, named, 0.0), axis=1, keepdims=True).astype(jnp.int32)
    pv = jnp.broadcast_to(pv, (blocks, 128))
    block_id = lax.broadcasted_iota(jnp.int32, (blocks, 128), 0)
    before = jnp.zeros((blocks, 128), jnp.int32)
    for k in range(blocks):
        before = before + jnp.where((pv == pv[k : k + 1]) & (block_id > k), 1, 0)
    slot = pv * 2 + before
    keys, keys_r, tiles, tiles_r = [], [], [], []
    for j in range(pairs):
        s0 = jnp.broadcast_to(slot[2 * j : 2 * j + 1], (8, 128))
        s1 = jnp.broadcast_to(slot[2 * j + 1 : 2 * j + 2], (8, 128))
        key = jnp.where(half == 0, s0, s1)
        at = pl.ds(128 * j, 128)
        rr = jnp.broadcast_to(row_ref[0, :, at], (8, 128))
        cc = jnp.broadcast_to(col_ref[0, :, at], (8, 128))
        ww = jnp.broadcast_to(wid_ref[0, :, at], (8, 128))
        tile = jnp.where(sub8 == 0, rr, jnp.where(sub8 == 1, cc, ww))
        keys.append(key)
        tiles.append(tile)
        keys_r.append(pltpu.roll(key, 64, 1))
        tiles_r.append(pltpu.roll(tile, 64, 1))
    for q in range(n_lon):
        want = 2 * q + half
        acc = jnp.zeros((8, 128), jnp.int32)
        for j in range(pairs):
            acc = jnp.where(keys[j] == want, tiles[j], acc)
            acc = jnp.where(keys_r[j] == want, tiles_r[j], acc)
        ask[q] = acc[0:4]

    pl.semaphore_wait(barrier, ndev - 1 + n_lon)

    def ask_copy(q, there):
        return pltpu.make_async_remote_copy(
            src_ref=ask.at[q], dst_ref=asked.at[there],
            send_sem=ask_send.at[q], recv_sem=ask_recv.at[there],
            device_id=dev(1 - p, a, q), device_id_type=MESH,
        )

    def send_ask(i, carry):
        q = lax.rem(b + i, n_lon)
        ask_copy(q, b).start()
        return carry

    lax.fori_loop(0, n_lon, send_ask, 0)

    ways = [(da, db) for da in (-1, 0, 1) for db in (-1, 0, 1) if (da, db) != (0, 0)]

    def exists(da, db):
        ok = None
        for pos, d, n in ((a, da, n_lat), (b, db, n_lon)):
            if d:
                c = (pos > 0) if d < 0 else (pos < n - 1)
                ok = c if ok is None else jnp.logical_and(ok, c)
        return ok

    def halo_copy(w, h):
        da, db = ways[w]
        src_rows = {-1: pl.ds(0, TOP), 0: pl.ds(0, 128), 1: pl.ds(128 - TOP, TOP)}[da]
        dst_rows = {-1: pl.ds(TOP + 128, TOP), 0: own, 1: pl.ds(0, TOP)}[da]
        if db == 0 and h["rows"] is not None:
            up, dn, got_up, got_dn = h["rows"]
            src, dst = (up, got_dn) if da < 0 else (dn, got_up)
        elif db == 0:
            src = h["body"].at[:, pl.ds(TOP if da < 0 else 128, TOP), :]
            dst = h["body"].at[:, dst_rows, :]
        else:
            into = h["cols"][1 if db > 0 else 2]
            src = h["cols"][0].at[src_rows, :]
            dst = into if h["flat"] else into.at[dst_rows, :]
        return pltpu.make_async_remote_copy(
            src_ref=src, dst_ref=dst, send_sem=h["send"].at[w], recv_sem=h["recv"].at[w],
            device_id=dev(p, a + da, b + db), device_id_type=MESH,
        )

    def ways_of(h):
        return [w for w, (da, db) in enumerate(ways) if not (h["flat"] and da and db)]

    def halo_send_all(h):
        for w in ways_of(h):
            @pl.when(exists(*ways[w]))
            def _(w=w):
                halo_copy(w, h).start()

    def halo_wait_recv(h):
        for w in ways_of(h):
            da, db = ways[w]

            @pl.when(exists(-da, -db))
            def _(w=w):
                halo_copy(w, h).wait_recv()

    def halo_wait_send(h):
        for w in ways_of(h):
            @pl.when(exists(*ways[w]))
            def _(w=w):
                halo_copy(w, h).wait_send()

    def halo_clear(h):
        for w in ways_of(h):
            da, db = ways[w]
            dst_rows = {-1: pl.ds(TOP + 128, TOP), 0: own, 1: pl.ds(0, TOP)}[da]
            if db == 0 and h["rows"] is not None:
                continue

            @pl.when(jnp.logical_not(exists(-da, -db)))
            def _(da=da, db=db, dst_rows=dst_rows):
                if db == 0:
                    h["body"][:, dst_rows, :] = jnp.zeros((levels, TOP, 128), F32)
                else:
                    buf = h["cols"][1 if db > 0 else 2]
                    if h["flat"]:
                        buf[...] = jnp.zeros((128, 128), F32)
                    else:
                        buf[dst_rows, :] = jnp.zeros((128 if da == 0 else TOP, 128), F32)

    def rows_of(group):
        spots, at = [], 0
        for f in range(*group):
            for k in range(levels):
                spots.append((f * levels + k, at, WIDTHS[f]))
                at += WIDTHS[f]
        return spots

    def pack_rows(group, h):
        up, dn = h["rows"][0:2]

        @pl.when(a > 0)
        def _():
            for c, at, w in rows_of(group):
                up[at : at + w, :] = x[c, TOP : TOP + w, :]

        @pl.when(a < n_lat - 1)
        def _():
            for c, at, w in rows_of(group):
                dn[at : at + w, :] = x[c, TOP + 128 - w : TOP + 128, :]

    def unpack_rows(group, h):
        got_up, got_dn = h["rows"][2:4]

        @pl.when(a > 0)
        def _():
            for c, at, w in rows_of(group):
                x[c, TOP - w : TOP, :] = got_up[at : at + w, :]

        @pl.when(a < n_lat - 1)
        def _():
            for c, at, w in rows_of(group):
                x[c, TOP + 128 : TOP + 128 + w, :] = got_dn[at : at + w, :]

    lane = lax.broadcasted_iota(jnp.int32, (rows_ext, 128), 1)
    lane_o = lax.broadcasted_iota(jnp.int32, (128, 128), 1)
    row_e = lax.broadcasted_iota(jnp.int32, (rows_ext, 128), 0)

    vargs = dict(
        rows=None, body=va, cols=(vpk, vpl, vpr), flat=False, send=v_send, recv=v_recv
    )
    hargs = (
        dict(
            rows=(to_up, to_dn, from_up, from_dn), cols=(pk, pkl, pkr), flat=False,
            send=halo_send, recv=halo_recv,
        ),
        dict(
            rows=(to_up2, to_dn2, from_up2, from_dn2), cols=(pk2, pkl2, pkr2), flat=True,
            send=halo2_send, recv=halo2_recv,
        ),
    )
    halo_clear(vargs)
    load_v.wait()
    vpk[...] = pack([va[k, own, :] for k in range(levels)], visc_windows(levels), lane_o)
    halo_send_all(vargs)
    halo_clear(hargs[0])
    halo_clear(hargs[1])

    load_f.wait()
    for f in range(6):
        v = fld[f].reshape(levels * 128, 128)
        hi = v.astype(BF16)
        lo = (v - hi.astype(F32)).astype(BF16)
        fcat[f, :, 0:128] = hi
        fcat[f, :, 128:256] = lo

    small[4].wait()
    cos_a = jnp.cos(ang_ref[0])
    sin_a = jnp.sin(ang_ref[0])
    colat = math.pi / 4.0 + ((a * 128 + row_e - TOP).astype(F32) + 0.5) * (
        math.pi / 2.0
    ) / (n_lat * 128)
    inv = 1.0 / jnp.sin(colat)
    gain = inv * inv
    inv_s[...] = inv
    gain_s[...] = gain
    is_own = (row_e >= TOP) & (row_e < TOP + 128)
    edge_lane = (lane == 0) | (lane == 127)
    ca = 2.0 + 2.0 * gain
    ca = ca - jnp.where((row_e == TOP) | (row_e == TOP + 127), 1.0, 0.0)
    ca = ca - jnp.where(edge_lane, gain, 0.0)
    rim = jnp.where((row_e == TOP - 1) | (row_e == TOP + 128), 1.0, 0.0)
    coef_a[...] = jnp.where(is_own, ca, rim)
    coef_h[...] = jnp.where(is_own & edge_lane, gain, 0.0)

    replies, answers = (reply0, reply1), (answer0, answer1)

    def rep_copy(g, q, there):
        return pltpu.make_async_remote_copy(
            src_ref=replies[g].at[q], dst_ref=answers[g].at[there],
            send_sem=rep_send.at[g * n_lon + q], recv_sem=rep_recv.at[g * n_lon + there],
            device_id=dev(1 - p, a, q), device_id_type=MESH,
        )

    sub_c = lax.broadcasted_iota(jnp.int32, (128, 256), 0)

    def serve(g, i, carry):
        pr = lax.rem(b // 2 + i, n_lon // 2)
        q0 = 2 * pr
        if g == 0:
            ask_copy(0, q0).wait_recv()
            ask_copy(0, q0 + 1).wait_recv()
        r0 = asked[q0]
        r1 = asked[q0 + 1]
        rr = jnp.concatenate([r0[0:1], r1[0:1]], axis=1)
        cc = jnp.concatenate([r0[1:2], r1[1:2]], axis=1)
        ww = jnp.concatenate([r0[2:3], r1[2:3]], axis=1)
        fa = ((ww >> 3).astype(F32) + 0.5) / WQ
        fo = ((ww & 7).astype(F32) + 0.5) / WQ
        cw = jnp.where(sub_c == cc, 1.0 - fo, jnp.where(sub_c == cc + 1, fo, 0.0)).astype(BF16)
        rw = jnp.where(sub_c == rr, 1.0 - fa, jnp.where(sub_c == rr + 1, fa, 0.0))
        cw2 = jnp.concatenate([cw, cw], axis=0)
        parts = []
        for f in range(*GROUPS[g]):
            v = jnp.dot(fcat[f], cw2, preferred_element_type=F32)
            parts.append(jnp.sum(v.reshape(levels, 128, 256) * rw[None], axis=1))
        res = jnp.concatenate(parts, axis=0)
        replies[g][q0] = res[:, 0:128]
        replies[g][q0 + 1] = res[:, 128:256]
        rep_copy(g, q0, b).start()
        rep_copy(g, q0 + 1, b).start()
        return carry

    lax.fori_loop(0, n_lon // 2, functools.partial(serve, 0), 0)
    small[5].wait()
    dest = dest_ref[0]
    sub_d = lax.broadcasted_iota(jnp.int32, (128, cells), 0)
    rm = jnp.where(sub_d == dest // 128, 1.0, 0.0).astype(BF16)
    cm = jnp.where(sub_d == dest % 128, 1.0, 0.0).astype(BF16)
    rmask[...] = rm
    cmask[:, 0:cells] = cm
    cmask[:, cells : 2 * cells] = cm
    nt = (((1,), (1,)), ((), ()))
    hit_s[...] = lax.dot_general(rm, cm, nt, preferred_element_type=F32)
    lax.fori_loop(0, n_lon // 2, functools.partial(serve, 1), 0)
    halo_wait_recv(vargs)
    vmerged = jnp.where(right_part(visc_windows(levels), lane), vpr[...], vpl[...])
    for k in range(levels):
        vh[k] = unpack(vmerged, visc_windows(levels)[k], lane)

    half_row = half[0:1]

    def fill(g):
        first_f, end_f = GROUPS[g]

        def wait_rep(q, carry):
            rep_copy(g, 0, q).wait_recv()
            return carry

        lax.fori_loop(0, n_lon, wait_rep, 0)
        got = [answers[g][q] for q in range(n_lon)]
        got_r = [pltpu.roll(v, 64, 1) for v in got]
        picked = []
        for j in range(pairs):
            key = keys[j][0:1]
            acc = jnp.zeros(((end_f - first_f) * levels, 128), F32)
            for q in range(n_lon):
                acc = jnp.where(key == 2 * q + half_row, got[q], acc)
                acc = jnp.where(key == 2 * q + 1 - half_row, got_r[q], acc)
            picked.append(acc)
        values = jnp.concatenate(picked, axis=1)
        fv = [values[f * levels : (f + 1) * levels] for f in range(end_f - first_f)]
        if g == 0:
            turned = [
                fv[0], cos_a * fv[1] + sin_a * fv[2], cos_a * fv[2] - sin_a * fv[1], fv[3],
            ]
        else:
            turned = [cos_a * fv[0] + sin_a * fv[1], cos_a * fv[1] - sin_a * fv[0]]
        hit = hit_s[...] > 0.5
        for f in range(first_f, end_f):
            v = turned[f - first_f]
            hi = v.astype(BF16)
            lo = (v - hi.astype(F32)).astype(BF16)
            left = []
            for k in range(levels):
                left.append(
                    jnp.concatenate(
                        [rmask[...] * hi[k : k + 1], rmask[...] * lo[k : k + 1]], axis=1
                    )
                )
            put = lax.dot_general(
                jnp.concatenate(left, axis=0), cmask[...], nt, preferred_element_type=F32
            )
            for k in range(levels):
                x[f * levels + k, own, :] = jnp.where(
                    hit, put[k * 128 : (k + 1) * 128], fld[f, k]
                )
        h = hargs[g]
        pack_rows(GROUPS[g], h)
        h["cols"][0][...] = pack(
            [x[c, own, :] for c in range(first_f * levels, end_f * levels)],
            windows(levels, GROUPS[g]), lane_o,
        )
        halo_send_all(h)

    fill(0)
    fill(1)
    halo_wait_recv(hargs[0])
    unpack_rows(GROUPS[0], hargs[0])
    spans = windows(levels, GROUPS[0])
    merged = jnp.where(right_part(spans, lane), pkr[...], pkl[...])
    for c, span in enumerate(spans):
        hx[c] = unpack(merged, span, lane)

    rows_ok = ((row_e >= TOP) | (a > 0)) & ((row_e < TOP + 128) | (a < n_lat - 1))
    lanes_ok = ((lane >= 64) | (b < n_lon - 1)) & ((lane < 64) | (b > 0))
    halo_ok = rows_ok & lanes_ok
    first, last = lane == 0, lane == 127

    def sides(body, rim):
        ra, rh = pltpu.roll(body, 127, 1), pltpu.roll(rim, 127, 1)
        la, lh = pltpu.roll(body, 1, 1), pltpu.roll(rim, 1, 1)
        return (
            jnp.where(last, rh, ra), jnp.where(first, lh, la),
            jnp.where(last, ra, rh), jnp.where(first, la, lh),
        )

    def next_row(v):
        return pltpu.roll(v, rows_ext - 1, 0)

    def prev_row(v):
        return pltpu.roll(v, 1, 0)

    def levels_sum(ref, base, k, index=slice(None)):
        total = None
        for d in (-1, 1):
            if 0 <= k + d < levels:
                v = ref[base + k + d, index, :]
                total = v if total is None else total + v
        return total

    def levels_diff(ref, base, k, index=slice(None)):
        up = ref[base + k + 1, index, :] if k + 1 < levels else 0.0
        down = ref[base + k - 1, index, :] if k > 0 else 0.0
        return up - down

    gain = gain_s[...]
    for f in range(3):
        for k in range(levels):
            c = f * levels + k
            body, rim = x[c], hx[c]
            r, l, rr, ll = sides(body, rim)
            mid = 4.0 + 2.0 * gain
            lap = next_row(body) + prev_row(body) + gain * (r + l) - mid * body
            lap = lap + levels_sum(x, f * levels, k)
            new = body + va[k] * lap
            lap_h = next_row(rim) + prev_row(rim) + gain * (rr + ll) - mid * rim
            lap_h = lap_h + levels_sum(hx, f * levels, k)
            new_h = rim + vh[k] * lap_h
            if f == 0:
                new = new + BUOYANCY * x[3 * levels + k]
                new_h = new_h + BUOYANCY * hx[3 * levels + k]
            st[c] = jnp.where(rows_ok, new, 0.0)
            sth[c] = jnp.where(halo_ok, new_h, 0.0)

    scale = -0.5 / (4.0 + 2.0 * gain)
    for k in range(levels):
        r, l, rr, ll = sides(st[2 * levels + k], sth[2 * levels + k])
        b1, h1 = st[levels + k], sth[levels + k]
        d = next_row(b1) - prev_row(b1) + inv_s[...] * (r - l) + levels_diff(st, 0, k)
        dh = next_row(h1) - prev_row(h1) + inv_s[...] * (rr - ll) + levels_diff(sth, 0, k)
        p1[k] = jnp.where(rows_ok, scale * d, 0.0)
        p1h[k] = jnp.where(halo_ok, scale * dh, 0.0)

    shape = mine.shape
    place = lax.broadcasted_iota(jnp.int32, shape, 0) * 128
    place = place + lax.broadcasted_iota(jnp.int32, shape, 1)
    tile = jnp.zeros(shape, F32)
    for k in range(levels):
        part = coef_a[...] * p1[k] + coef_h[...] * p1h[k]
        part = part + jnp.where(is_own, levels_sum(p1, 0, k), 0.0)
        total = jnp.sum(jnp.sum(part, axis=0, keepdims=True), axis=1, keepdims=True)
        tile = tile + jnp.where(place == me * levels + k, total * (1.0 / 128.0), 0.0)
    mine[...] = tile

    def sum_copy(t, there, i):
        return pltpu.make_async_remote_copy(
            src_ref=mine, dst_ref=sums.at[there],
            send_sem=sum_send.at[i], recv_sem=sum_recv.at[there],
            device_id=dev(p, t // n_lon, lax.rem(t, n_lon)), device_id_type=MESH,
        )

    def send_sum(i, carry):
        sum_copy(lax.rem(me + i, ndev), me, i).start()
        return carry

    lax.fori_loop(1, ndev, send_sum, 0)

    gain_o = gain_s[own, :]
    inv_o = inv_s[own, :]
    first_o, last_o = lane_o == 0, lane_o == 127

    def sides_own(body, rim):
        r = jnp.where(last_o, pltpu.roll(rim, 127, 1), pltpu.roll(body, 127, 1))
        l = jnp.where(first_o, pltpu.roll(rim, 1, 1), pltpu.roll(body, 1, 1))
        return r, l

    halo_wait_recv(hargs[1])
    unpack_rows(GROUPS[1], hargs[1])
    spans = windows(levels, GROUPS[1])
    merged = jnp.where(right_part(spans, lane_o), pkr2[...], pkl2[...])
    for c, span in enumerate(spans):
        hx[4 * levels + c, own, :] = unpack(merged, span, lane_o)
    for f in range(3, 6):
        for k in range(levels):
            c = f * levels + k
            body = x[c]
            mid = body[TOP : TOP + 128]
            r, l = sides_own(mid, hx[c, own, :])
            lap = next_row(body)[TOP : TOP + 128] + prev_row(body)[TOP : TOP + 128]
            lap = lap + gain_o * (r + l) - (4.0 + 2.0 * gain_o) * mid
            lap = lap + levels_sum(x, f * levels, k, own)
            onew[f, k] = mid + va[k, own, :] * lap
    store_late = pltpu.make_async_copy(
        onew.at[pl.ds(3, 3)], out_ref.at[pl.ds(3, 3)], out_sem.at[0]
    )
    store_late.start()
    for k in range(levels):
        body = p1[k]
        mid = body[TOP : TOP + 128]
        r, l = sides_own(mid, p1h[k, own, :])
        diff = next_row(body)[TOP : TOP + 128] - prev_row(body)[TOP : TOP + 128]
        onew[0, k] = st[k, own, :] - 0.5 * levels_diff(p1, 0, k, own)
        onew[1, k] = st[levels + k, own, :] - 0.5 * diff
        onew[2, k] = st[2 * levels + k, own, :] - 0.5 * inv_o * (r - l)

    store_new = pltpu.make_async_copy(
        onew.at[pl.ds(0, 3)], out_ref.at[pl.ds(0, 3)], out_sem.at[1]
    )
    store_p = pltpu.make_async_copy(p1.at[:, own, :], press_ref, out_sem.at[2])
    store_new.start()
    store_p.start()

    for c in load_o:
        c.wait()

    def take_sum(i, total):
        s = lax.rem(me + i, ndev)
        sum_copy(me, s, 0).wait_recv()
        return total + sums[s]

    vec = lax.fori_loop(1, ndev, take_sum, mine[...])

    def coarse(t, k):
        prod = opr[t, k] * vec
        return jnp.sum(jnp.sum(prod, axis=0, keepdims=True), axis=1, keepdims=True)

    zero = jnp.zeros((1, 1), F32)
    there = (None, a > 0, a < n_lat - 1, b > 0, b < n_lon - 1)
    for t in range(5):
        for k in range(levels):
            c = coarse(t, k)
            c = c if t == 0 else jnp.where(there[t], c, zero)
            cvals[t * levels + k : t * levels + k + 1, :] = jnp.broadcast_to(c, (1, 128))
    store_c = pltpu.make_async_copy(cvals, cv_ref, out_sem.at[3])
    store_c.start()

    def end_lon(q, carry):
        ask_copy(q, b).wait_send()
        rep_copy(0, q, b).wait_send()
        rep_copy(1, q, b).wait_send()
        return carry

    lax.fori_loop(0, n_lon, end_lon, 0)
    halo_wait_send(vargs)
    halo_wait_send(hargs[0])
    halo_wait_send(hargs[1])

    def end_sum(i, carry):
        sum_copy(me, me, i).wait_send()
        return carry

    lax.fori_loop(1, ndev, end_sum, 0)
    store_late.wait()
    store_new.wait()
    store_p.wait()
    store_c.wait()


def finish(
    dims, part_f, part_p, cv_in, out_ref, press_ref, new, press, cvals, in_sem, out_sem
):
    n_lat, levels = dims
    a = lax.axis_index("lat")
    late, early = pl.ds(3, 3), pl.ds(0, 3)
    loads = [
        pltpu.make_async_copy(src, dst, in_sem.at[i])
        for i, (src, dst) in enumerate(
            (
                (part_f.at[late], new.at[late]), (part_f.at[early], new.at[early]),
                (part_p, press), (cv_in, cvals),
            )
        )
    ]
    for c in loads:
        c.start()
    row = lax.broadcasted_iota(jnp.int32, (128, 128), 0)
    lane = lax.broadcasted_iota(jnp.int32, (128, 128), 1)
    colat = math.pi / 4.0 + ((a * 128 + row).astype(F32) + 0.5) * (math.pi / 2.0) / (
        n_lat * 128
    )
    inv = 1.0 / jnp.sin(colat)
    stores = [
        pltpu.make_async_copy(new.at[late], out_ref.at[0, late], out_sem.at[0]),
        pltpu.make_async_copy(new.at[early], out_ref.at[0, early], out_sem.at[1]),
        pltpu.make_async_copy(press, press_ref.at[0], out_sem.at[2]),
    ]
    loads[0].wait()
    stores[0].start()
    for c in loads[1:]:
        c.wait()

    def value(t, k):
        at = t * levels + k
        return cvals[at : at + 1, :]

    for k in range(levels):
        c = value(0, k)
        press[k] = press[k] + c
        high = value(0, k + 1) if k + 1 < levels else 0.0
        low = value(0, k - 1) if k > 0 else 0.0
        new[0, k] = new[0, k] - 0.5 * (high - low)
        fix = jnp.where(row == 0, c - value(1, k), 0.0)
        fix = jnp.where(row == 127, value(2, k) - c, fix)
        new[1, k] = new[1, k] - 0.5 * fix
        fix = jnp.where(lane == 0, c - value(3, k), 0.0)
        fix = jnp.where(lane == 127, value(4, k) - c, fix)
        new[2, k] = new[2, k] - 0.5 * inv * fix
    stores[1].start()
    stores[2].start()
    for c in stores:
        c.wait()


def solution(mesh):
    n_lat, n_lon = mesh.shape["lat"], mesh.shape["lon"]

    def shards(fields, viscosity, partner, src_row, src_col, weight_id, border_angle, dest_cell):
        levels = fields.shape[2]
        blocks = partner.shape[2]
        channels = 6 * levels
        ext = 128 + 2 * TOP
        ndev = n_lat * n_lon
        cells = src_row.shape[2]
        oper = jnp.asarray(coarse_operator(levels, n_lat, n_lon))
        anyw = pl.BlockSpec(memory_space=pl.ANY)
        v = lambda *s: pltpu.VMEM(s, F32)
        vi = lambda *s: pltpu.VMEM(s, jnp.int32)
        sem = lambda n: pltpu.SemaphoreType.DMA((n,))
        rows0, rows1 = 11 * levels, 2 * levels
        used = oper.shape[2]
        part_f, part_p, cvals = pl.pallas_call(
            functools.partial(kernel, (n_lat, n_lon, levels, blocks)),
            out_shape=(
                jax.ShapeDtypeStruct(fields.shape[1:], F32),
                jax.ShapeDtypeStruct(viscosity.shape[1:], F32),
                jax.ShapeDtypeStruct((5 * levels, 128), F32),
            ),
            in_specs=[anyw] * 9,
            out_specs=(anyw, anyw, anyw),
            scratch_shapes=[
                vi(1, 1, blocks), vi(1, 1, cells), vi(1, 1, cells), vi(1, 1, cells),
                v(1, 1, cells), vi(1, 1, cells),
                v(6, levels, 128, 128),
                pltpu.VMEM((6, levels * 128, 256), BF16),
                vi(n_lon, 4, 128), vi(n_lon, 4, 128),
                v(n_lon, 4 * levels, 128), v(n_lon, 4 * levels, 128),
                v(n_lon, 2 * levels, 128), v(n_lon, 2 * levels, 128),
                v(channels, ext, 128),
                v(channels, ext, 128),
                v(128, 128), v(ext, 128), v(ext, 128),
                v(128, 128), v(128, 128), v(128, 128),
                v(rows0, 128), v(rows0, 128), v(rows0, 128), v(rows0, 128),
                v(rows1, 128), v(rows1, 128), v(rows1, 128), v(rows1, 128),
                v(levels, ext, 128), v(levels, ext, 128),
                v(128, 128), v(ext, 128), v(ext, 128),
                v(ext, 128), v(ext, 128), v(ext, 128), v(ext, 128),
                v(3 * levels, ext, 128), v(3 * levels, ext, 128),
                v(levels, ext, 128), v(levels, ext, 128),
                v(128, 128),
                pltpu.VMEM((128, cells), BF16),
                pltpu.VMEM((128, 2 * cells), BF16),
                v(5, levels, used, 128),
                v(ndev, used, 128),
                v(used, 128),
                v(6, levels, 128, 128),
                v(5 * levels, 128),
                sem(8), sem(5), sem(4),
                sem(n_lon), sem(n_lon), sem(2 * n_lon), sem(2 * n_lon),
                sem(8), sem(8), sem(8), sem(8), sem(8), sem(8), sem(ndev), sem(ndev),
            ],
            compiler_params=pltpu.CompilerParams(
                collective_id=0, has_side_effects=True, vmem_limit_bytes=60 * 1024 * 1024
            ),
            name="shell_step",
        )(
            partner.reshape(1, 1, blocks), src_row, src_col, weight_id, border_angle, dest_cell,
            fields, viscosity, oper,
        )
        return pl.pallas_call(
            functools.partial(finish, (n_lat, levels)),
            out_shape=(
                jax.ShapeDtypeStruct(fields.shape, F32),
                jax.ShapeDtypeStruct(viscosity.shape, F32),
            ),
            in_specs=[anyw] * 3,
            out_specs=(anyw, anyw),
            scratch_shapes=[
                v(6, levels, 128, 128), v(levels, 128, 128), v(5 * levels, 128), sem(4), sem(3),
            ],
            compiler_params=pltpu.CompilerParams(vmem_limit_bytes=60 * 1024 * 1024),
            name="finish",
        )(part_f, part_p, cvals)

    return jax.shard_map(
        shards,
        mesh=mesh,
        in_specs=(
            P("panel", None, None, "lat", "lon"),
            P("panel", None, "lat", "lon"),
            P("panel", "lat", "lon", None),
            P("panel", "lat", "lon"),
            P("panel", "lat", "lon"),
            P("panel", "lat", "lon"),
            P("panel", "lat", "lon"),
            P("panel", "lat", "lon"),
        ),
        out_specs=(P("panel", None, None, "lat", "lon"), P("panel", None, "lat", "lon")),
        check_vma=False,
    )
```

```python
import functools
import math

import jax
import jax.numpy as jnp
import numpy as np
from jax import lax
from jax.experimental import pallas as pl
from jax.experimental.pallas import tpu as pltpu
from jax.sharding import PartitionSpec as P

MESH = pl.DeviceIdType.MESH
WQ = 8
BUOYANCY = 0.5
TOP = 8
F32 = jnp.float32
BF16 = jnp.bfloat16


def coarse_operator(levels, n_lat, n_lon):
    def table(n):
        m = np.arange(n, dtype=np.float64)
        norm = np.sqrt(np.where(m > 0, 2.0, 1.0) / n)
        q = norm[:, None] * np.cos(np.pi * m[:, None] * (m[None, :] + 0.5) / n)
        return q, 4.0 * np.sin(np.pi * m / (2.0 * n)) ** 2

    qr, er = table(levels)
    qa, ea = table(n_lat)
    qo, eo = table(n_lon)
    inv = 1.0 / (
        ea[:, None, None] + eo[None, :, None] + er[None, None, :] + 1.0 / (n_lat * n_lon)
    )
    q = np.einsum("ax,oy,rz->aorxyz", qa, qo, qr).reshape(inv.size, inv.size)
    full = (q.T * inv.reshape(-1)) @ q / math.sqrt(n_lat * n_lon)
    count = inv.size
    used = -(-count // 128)
    wide = np.zeros((count, used * 128), np.float32)
    wide[:, :count] = full
    return wide.reshape(n_lat * n_lon, levels, used, 128)


GROUPS = ((0, 4), (4, 6))
WIDTHS = (3, 3, 3, 3, 1, 1)


def windows(levels, group):
    spans, at = [], 0
    for width in WIDTHS[group[0] : group[1]]:
        for _ in range(levels):
            spans.append((at + width, width))
            at += 2 * width
    return spans


def visc_windows(levels):
    return [(6 * k + 3, 3) for k in range(levels)]


def pack(tiles, spans, lane):
    packed = None
    for tile, (centre, width) in zip(tiles, spans):
        moved = pltpu.roll(tile, centre, 1)
        inside = (lane >= centre - width) & (lane < centre + width)
        packed = jnp.where(inside, moved, 0.0 if packed is None else packed)
    return packed


def right_part(spans, lane):
    mask = jnp.zeros(lane.shape, jnp.int32)
    for centre, width in spans:
        mask = jnp.where((lane >= centre) & (lane < centre + width), 1, mask)
    return mask > 0


def kernel(
    dims,
    partner_in, row_in, col_in, wid_in, ang_in, dest_in, fields_ref, visc_ref, oper_ref,
    out_ref, press_ref, cv_ref,
    partner_ref, row_ref, col_ref, wid_ref, ang_ref, dest_ref,
    fld, fcat, ask, asked, reply0, answer0, reply1, answer1, x, hx,
    pk, pkl, pkr, pk2, pkl2, pkr2, to_up, to_dn, from_up, from_dn,
    to_up2, to_dn2, from_up2, from_dn2, va, vh, vpk, vpl, vpr,
    inv_s, gain_s, coef_a, coef_h, st, sth, p1, p1h, hit_s, rmask, cmask,
    opr, sums, mine, onew, cvals,
    in_sem, op_sem, out_sem, ask_send, ask_recv, rep_send, rep_recv,
    halo_send, halo_recv, halo2_send, halo2_recv, v_send, v_recv, sum_send, sum_recv,
):
    n_lat, n_lon, levels, blocks = dims
    ndev = n_lat * n_lon
    channels = 6 * levels
    rows_ext = 128 + 2 * TOP
    pairs = blocks // 2
    cells = blocks * 64
    p = lax.axis_index("panel")
    a = lax.axis_index("lat")
    b = lax.axis_index("lon")
    me = a * n_lon + b
    own = pl.ds(TOP, 128)

    def dev(panel, lat, lon):
        return {"panel": panel, "lat": lat, "lon": lon}

    load_f = pltpu.make_async_copy(fields_ref.at[0], fld, in_sem.at[0])
    load_v = pltpu.make_async_copy(visc_ref.at[0], va.at[:, own, :], in_sem.at[1])
    small = [
        pltpu.make_async_copy(src, dst, in_sem.at[2 + i])
        for i, (src, dst) in enumerate(
            (
                (partner_in, partner_ref), (row_in, row_ref), (col_in, col_ref),
                (wid_in, wid_ref), (ang_in, ang_ref), (dest_in, dest_ref),
            )
        )
    ]
    for c in small:
        c.start()
    load_f.start()
    load_v.start()
    targets = (
        me,
        jnp.maximum(a - 1, 0) * n_lon + b,
        jnp.minimum(a + 1, n_lat - 1) * n_lon + b,
        a * n_lon + jnp.maximum(b - 1, 0),
        a * n_lon + jnp.minimum(b + 1, n_lon - 1),
    )
    load_o = [
        pltpu.make_async_copy(oper_ref.at[t], opr.at[i], op_sem.at[i])
        for i, t in enumerate(targets)
    ]
    for c in load_o:
        c.start()

    barrier = pltpu.get_barrier_semaphore()

    def greet(i, carry):
        t = lax.rem(me + i, ndev)
        pl.semaphore_signal(
            barrier, inc=1, device_id=dev(p, t // n_lon, lax.rem(t, n_lon)), device_id_type=MESH
        )
        return carry

    lax.fori_loop(1, ndev, greet, 0)

    def greet_other(i, carry):
        pl.semaphore_signal(barrier, inc=1, device_id=dev(1 - p, a, i), device_id_type=MESH)
        return carry

    lax.fori_loop(0, n_lon, greet_other, 0)

    lane8 = lax.broadcasted_iota(jnp.int32, (8, 128), 1)
    sub8 = lax.broadcasted_iota(jnp.int32, (8, 128), 0)
    half = lane8 // 64
    zero_rows = jnp.zeros((6 * levels, TOP, 128), F32)
    x[:, 0:TOP, :] = zero_rows
    x[:, TOP + 128 : rows_ext, :] = zero_rows
    for c in small[:4]:
        c.wait()
    named = jnp.broadcast_to(partner_ref[0], (blocks, blocks)).astype(F32)
    diag = lax.broadcasted_iota(jnp.int32, (blocks, blocks), 0) == lax.broadcasted_iota(
        jnp.int32, (blocks, blocks), 1
    )
    pv = jnp.sum(jnp.where(diag, named, 0.0), axis=1, keepdims=True).astype(jnp.int32)
    pv = jnp.broadcast_to(pv, (blocks, 128))
    block_id = lax.broadcasted_iota(jnp.int32, (blocks, 128), 0)
    before = jnp.zeros((blocks, 128), jnp.int32)
    for k in range(blocks):
        before = before + jnp.where((pv == pv[k : k + 1]) & (block_id > k), 1, 0)
    slot = pv * 2 + before
    keys, keys_r, tiles, tiles_r = [], [], [], []
    for j in range(pairs):
        s0 = jnp.broadcast_to(slot[2 * j : 2 * j + 1], (8, 128))
        s1 = jnp.broadcast_to(slot[2 * j + 1 : 2 * j + 2], (8, 128))
        key = jnp.where(half == 0, s0, s1)
        at = pl.ds(128 * j, 128)
        rr = jnp.broadcast_to(row_ref[0, :, at], (8, 128))
        cc = jnp.broadcast_to(col_ref[0, :, at], (8, 128))
        ww = jnp.broadcast_to(wid_ref[0, :, at], (8, 128))
        tile = jnp.where(sub8 == 0, rr, jnp.where(sub8 == 1, cc, ww))
        keys.append(key)
        tiles.append(tile)
        keys_r.append(pltpu.roll(key, 64, 1))
        tiles_r.append(pltpu.roll(tile, 64, 1))
    for q in range(n_lon):
        want = 2 * q + half
        acc = jnp.zeros((8, 128), jnp.int32)
        for j in range(pairs):
            acc = jnp.where(keys[j] == want, tiles[j], acc)
            acc = jnp.where(keys_r[j] == want, tiles_r[j], acc)
        ask[q] = acc[0:4]

    pl.semaphore_wait(barrier, ndev - 1 + n_lon)

    def ask_copy(q, there):
        return pltpu.make_async_remote_copy(
            src_ref=ask.at[q], dst_ref=asked.at[there],
            send_sem=ask_send.at[q], recv_sem=ask_recv.at[there],
            device_id=dev(1 - p, a, q), device_id_type=MESH,
        )

    def send_ask(i, carry):
        q = lax.rem(b + i, n_lon)
        ask_copy(q, b).start()
        return carry

    lax.fori_loop(0, n_lon, send_ask, 0)

    ways = [(da, db) for da in (-1, 0, 1) for db in (-1, 0, 1) if (da, db) != (0, 0)]

    def exists(da, db):
        ok = None
        for pos, d, n in ((a, da, n_lat), (b, db, n_lon)):
            if d:
                c = (pos > 0) if d < 0 else (pos < n - 1)
                ok = c if ok is None else jnp.logical_and(ok, c)
        return ok

    def halo_copy(w, h):
        da, db = ways[w]
        src_rows = {-1: pl.ds(0, TOP), 0: pl.ds(0, 128), 1: pl.ds(128 - TOP, TOP)}[da]
        dst_rows = {-1: pl.ds(TOP + 128, TOP), 0: own, 1: pl.ds(0, TOP)}[da]
        if db == 0 and h["rows"] is not None:
            up, dn, got_up, got_dn = h["rows"]
            src, dst = (up, got_dn) if da < 0 else (dn, got_up)
        elif db == 0:
            src = h["body"].at[:, pl.ds(TOP if da < 0 else 128, TOP), :]
            dst = h["body"].at[:, dst_rows, :]
        else:
            into = h["cols"][1 if db > 0 else 2]
            src = h["cols"][0].at[src_rows, :]
            dst = into if h["flat"] else into.at[dst_rows, :]
        return pltpu.make_async_remote_copy(
            src_ref=src, dst_ref=dst, send_sem=h["send"].at[w], recv_sem=h["recv"].at[w],
            device_id=dev(p, a + da, b + db), device_id_type=MESH,
        )

    def ways_of(h):
        return [w for w, (da, db) in enumerate(ways) if not (h["flat"] and da and db)]

    def halo_send_all(h):
        for w in ways_of(h):
            @pl.when(exists(*ways[w]))
            def _(w=w):
                halo_copy(w, h).start()

    def halo_wait_recv(h):
        for w in ways_of(h):
            da, db = ways[w]

            @pl.when(exists(-da, -db))
            def _(w=w):
                halo_copy(w, h).wait_recv()

    def halo_wait_send(h):
        for w in ways_of(h):
            @pl.when(exists(*ways[w]))
            def _(w=w):
                halo_copy(w, h).wait_send()

    def halo_clear(h):
        for w in ways_of(h):
            da, db = ways[w]
            dst_rows = {-1: pl.ds(TOP + 128, TOP), 0: own, 1: pl.ds(0, TOP)}[da]
            if db == 0 and h["rows"] is not None:
                continue

            @pl.when(jnp.logical_not(exists(-da, -db)))
            def _(da=da, db=db, dst_rows=dst_rows):
                if db == 0:
                    h["body"][:, dst_rows, :] = jnp.zeros((levels, TOP, 128), F32)
                else:
                    buf = h["cols"][1 if db > 0 else 2]
                    if h["flat"]:
                        buf[...] = jnp.zeros((128, 128), F32)
                    else:
                        buf[dst_rows, :] = jnp.zeros((128 if da == 0 else TOP, 128), F32)

    def rows_of(group):
        spots, at = [], 0
        for f in range(*group):
            for k in range(levels):
                spots.append((f * levels + k, at, WIDTHS[f]))
                at += WIDTHS[f]
        return spots

    def pack_rows(group, h):
        up, dn = h["rows"][0:2]

        @pl.when(a > 0)
        def _():
            for c, at, w in rows_of(group):
                up[at : at + w, :] = x[c, TOP : TOP + w, :]

        @pl.when(a < n_lat - 1)
        def _():
            for c, at, w in rows_of(group):
                dn[at : at + w, :] = x[c, TOP + 128 - w : TOP + 128, :]

    def unpack_rows(group, h):
        got_up, got_dn = h["rows"][2:4]

        @pl.when(a > 0)
        def _():
            for c, at, w in rows_of(group):
                x[c, TOP - w : TOP, :] = got_up[at : at + w, :]

        @pl.when(a < n_lat - 1)
        def _():
            for c, at, w in rows_of(group):
                x[c, TOP + 128 : TOP + 128 + w, :] = got_dn[at : at + w, :]

    lane = lax.broadcasted_iota(jnp.int32, (rows_ext, 128), 1)
    lane_o = lax.broadcasted_iota(jnp.int32, (128, 128), 1)
    row_e = lax.broadcasted_iota(jnp.int32, (rows_ext, 128), 0)

    vargs = dict(
        rows=None, body=va, cols=(vpk, vpl, vpr), flat=False, send=v_send, recv=v_recv
    )
    hargs = (
        dict(
            rows=(to_up, to_dn, from_up, from_dn), cols=(pk, pkl, pkr), flat=False,
            send=halo_send, recv=halo_recv,
        ),
        dict(
            rows=(to_up2, to_dn2, from_up2, from_dn2), cols=(pk2, pkl2, pkr2), flat=True,
            send=halo2_send, recv=halo2_recv,
        ),
    )
    halo_clear(vargs)
    load_v.wait()
    vpk[...] = pack([va[k, own, :] for k in range(levels)], visc_windows(levels), lane_o)
    halo_send_all(vargs)
    halo_clear(hargs[0])
    halo_clear(hargs[1])

    load_f.wait()
    for f in range(6):
        v = fld[f].reshape(levels * 128, 128)
        hi = v.astype(BF16)
        lo = (v - hi.astype(F32)).astype(BF16)
        fcat[f, :, 0:128] = hi
        fcat[f, :, 128:256] = lo

    small[4].wait()
    cos_a = jnp.cos(ang_ref[0])
    sin_a = jnp.sin(ang_ref[0])
    colat = math.pi / 4.0 + ((a * 128 + row_e - TOP).astype(F32) + 0.5) * (
        math.pi / 2.0
    ) / (n_lat * 128)
    inv = 1.0 / jnp.sin(colat)
    gain = inv * inv
    inv_s[...] = inv
    gain_s[...] = gain
    is_own = (row_e >= TOP) & (row_e < TOP + 128)
    edge_lane = (lane == 0) | (lane == 127)
    ca = 2.0 + 2.0 * gain
    ca = ca - jnp.where((row_e == TOP) | (row_e == TOP + 127), 1.0, 0.0)
    ca = ca - jnp.where(edge_lane, gain, 0.0)
    rim = jnp.where((row_e == TOP - 1) | (row_e == TOP + 128), 1.0, 0.0)
    coef_a[...] = jnp.where(is_own, ca, rim)
    slot6 = lane % 6
    at_west, at_east = slot6 == 2, slot6 == 3
    coef_h[...] = jnp.where(is_own & (at_west | at_east), gain, 0.0)

    replies, answers = (reply0, reply1), (answer0, answer1)

    def rep_copy(g, q, there):
        return pltpu.make_async_remote_copy(
            src_ref=replies[g].at[q], dst_ref=answers[g].at[there],
            send_sem=rep_send.at[g * n_lon + q], recv_sem=rep_recv.at[g * n_lon + there],
            device_id=dev(1 - p, a, q), device_id_type=MESH,
        )

    sub_c = lax.broadcasted_iota(jnp.int32, (128, 256), 0)

    def serve(g, i, carry):
        pr = lax.rem(b // 2 + i, n_lon // 2)
        q0 = 2 * pr
        if g == 0:
            ask_copy(0, q0).wait_recv()
            ask_copy(0, q0 + 1).wait_recv()
        r0 = asked[q0]
        r1 = asked[q0 + 1]
        rr = jnp.concatenate([r0[0:1], r1[0:1]], axis=1)
        cc = jnp.concatenate([r0[1:2], r1[1:2]], axis=1)
        ww = jnp.concatenate([r0[2:3], r1[2:3]], axis=1)
        fa = ((ww >> 3).astype(F32) + 0.5) / WQ
        fo = ((ww & 7).astype(F32) + 0.5) / WQ
        cw = jnp.where(sub_c == cc, 1.0 - fo, jnp.where(sub_c == cc + 1, fo, 0.0)).astype(BF16)
        rw = jnp.where(sub_c == rr, 1.0 - fa, jnp.where(sub_c == rr + 1, fa, 0.0))
        cw2 = jnp.concatenate([cw, cw], axis=0)
        parts = []
        for f in range(*GROUPS[g]):
            v = jnp.dot(fcat[f], cw2, preferred_element_type=F32)
            parts.append(jnp.sum(v.reshape(levels, 128, 256) * rw[None], axis=1))
        res = jnp.concatenate(parts, axis=0)
        replies[g][q0] = res[:, 0:128]
        replies[g][q0 + 1] = res[:, 128:256]
        rep_copy(g, q0, b).start()
        rep_copy(g, q0 + 1, b).start()
        return carry

    lax.fori_loop(0, n_lon // 2, functools.partial(serve, 0), 0)
    small[5].wait()
    dest = dest_ref[0]
    sub_d = lax.broadcasted_iota(jnp.int32, (128, cells), 0)
    rm = jnp.where(sub_d == dest // 128, 1.0, 0.0).astype(BF16)
    cm = jnp.where(sub_d == dest % 128, 1.0, 0.0).astype(BF16)
    rmask[...] = rm
    cmask[:, 0:cells] = cm
    cmask[:, cells : 2 * cells] = cm
    nt = (((1,), (1,)), ((), ()))
    hit_s[...] = lax.dot_general(rm, cm, nt, preferred_element_type=F32)
    lax.fori_loop(0, n_lon // 2, functools.partial(serve, 1), 0)
    halo_wait_recv(vargs)
    vmerged = jnp.where(right_part(visc_windows(levels), lane), vpr[...], vpl[...])
    span_f = 6 * levels
    vh[...] = jnp.where(
        lane < span_f, vmerged,
        jnp.where(
            lane < 2 * span_f, pltpu.roll(vmerged, span_f, 1), pltpu.roll(vmerged, 2 * span_f, 1)
        ),
    )

    half_row = half[0:1]

    def fill(g):
        first_f, end_f = GROUPS[g]

        def wait_rep(q, carry):
            rep_copy(g, 0, q).wait_recv()
            return carry

        lax.fori_loop(0, n_lon, wait_rep, 0)
        got = [answers[g][q] for q in range(n_lon)]
        got_r = [pltpu.roll(v, 64, 1) for v in got]
        picked = []
        for j in range(pairs):
            key = keys[j][0:1]
            acc = jnp.zeros(((end_f - first_f) * levels, 128), F32)
            for q in range(n_lon):
                acc = jnp.where(key == 2 * q + half_row, got[q], acc)
                acc = jnp.where(key == 2 * q + 1 - half_row, got_r[q], acc)
            picked.append(acc)
        values = jnp.concatenate(picked, axis=1)
        fv = [values[f * levels : (f + 1) * levels] for f in range(end_f - first_f)]
        if g == 0:
            turned = [
                fv[0], cos_a * fv[1] + sin_a * fv[2], cos_a * fv[2] - sin_a * fv[1], fv[3],
            ]
        else:
            turned = [cos_a * fv[0] + sin_a * fv[1], cos_a * fv[1] - sin_a * fv[0]]
        hit = hit_s[...] > 0.5
        for f in range(first_f, end_f):
            v = turned[f - first_f]
            hi = v.astype(BF16)
            lo = (v - hi.astype(F32)).astype(BF16)
            left = []
            for k in range(levels):
                left.append(
                    jnp.concatenate(
                        [rmask[...] * hi[k : k + 1], rmask[...] * lo[k : k + 1]], axis=1
                    )
                )
            put = lax.dot_general(
                jnp.concatenate(left, axis=0), cmask[...], nt, preferred_element_type=F32
            )
            for k in range(levels):
                x[f * levels + k, own, :] = jnp.where(
                    hit, put[k * 128 : (k + 1) * 128], fld[f, k]
                )
        h = hargs[g]
        pack_rows(GROUPS[g], h)
        h["cols"][0][...] = pack(
            [x[c, own, :] for c in range(first_f * levels, end_f * levels)],
            windows(levels, GROUPS[g]), lane_o,
        )
        halo_send_all(h)

    fill(0)
    fill(1)
    halo_wait_recv(hargs[0])
    unpack_rows(GROUPS[0], hargs[0])
    spans = windows(levels, GROUPS[0])
    merged = jnp.where(right_part(spans, lane), pkr[...], pkl[...])
    hx[...] = merged
    own_edges = jnp.concatenate(
        [
            pack([x[c, 0:TOP, :] for c in range(4 * levels)], spans, lane8),
            pk[...],
            pack([x[c, TOP + 128 : rows_ext, :] for c in range(4 * levels)], spans, lane8),
        ],
        axis=0,
    )

    rows_ok = ((row_e >= TOP) | (a > 0)) & ((row_e < TOP + 128) | (a < n_lat - 1))
    lanes_ok = ((slot6 >= 3) | (b > 0)) & ((slot6 < 3) | (b < n_lon - 1))
    halo_ok = rows_ok & lanes_ok
    level = (lane // 6) % levels
    first, last = lane == 0, lane == 127

    def sides(body, strip, centre, at_first, at_last):
        r = jnp.where(
            at_last, pltpu.roll(strip, (127 - centre) % 128, 1), pltpu.roll(body, 127, 1)
        )
        l = jnp.where(
            at_first, pltpu.roll(strip, (129 - centre) % 128, 1), pltpu.roll(body, 1, 1)
        )
        return r, l

    def strip_sides(strip, edges):
        r = jnp.where(at_west, pltpu.roll(edges, 127, 1), pltpu.roll(strip, 127, 1))
        l = jnp.where(at_east, pltpu.roll(edges, 1, 1), pltpu.roll(strip, 1, 1))
        return r, l

    def strip_levels(strip):
        up = jnp.where(level < levels - 1, pltpu.roll(strip, 122, 1), 0.0)
        down = jnp.where(level > 0, pltpu.roll(strip, 6, 1), 0.0)
        return up, down

    def next_row(v):
        return pltpu.roll(v, rows_ext - 1, 0)

    def prev_row(v):
        return pltpu.roll(v, 1, 0)

    def levels_sum(ref, base, k, index=slice(None)):
        total = None
        for d in (-1, 1):
            if 0 <= k + d < levels:
                v = ref[base + k + d, index, :]
                total = v if total is None else total + v
        return total

    def levels_diff(ref, base, k, index=slice(None)):
        up = ref[base + k + 1, index, :] if k + 1 < levels else 0.0
        down = ref[base + k - 1, index, :] if k > 0 else 0.0
        return up - down

    gain = gain_s[...]
    mid = 4.0 + 2.0 * gain
    for f in range(3):
        for k in range(levels):
            c = f * levels + k
            body = x[c]
            r, l = sides(body, hx[...], spans[c][0], first, last)
            lap = next_row(body) + prev_row(body) + gain * (r + l) - mid * body
            lap = lap + levels_sum(x, f * levels, k)
            new = body + va[k] * lap
            if f == 0:
                new = new + BUOYANCY * x[3 * levels + k]
            st[c] = jnp.where(rows_ok, new, 0.0)
    strip = hx[...]
    r, l = strip_sides(strip, own_edges)
    up, down = strip_levels(strip)
    lap = next_row(strip) + prev_row(strip) + gain * (r + l) - mid * strip + (up + down)
    new = strip + vh[...] * lap
    warm = pltpu.roll(strip, 128 - 3 * span_f, 1)
    new = new + jnp.where(lane < span_f, BUOYANCY * warm, 0.0)
    sth[...] = jnp.where(halo_ok & (lane < 3 * span_f), new, 0.0)

    scale = -0.5 / mid
    for k in range(levels):
        r, l = sides(st[2 * levels + k], sth[...], spans[2 * levels + k][0], first, last)
        b1 = st[levels + k]
        d = next_row(b1) - prev_row(b1) + inv_s[...] * (r - l) + levels_diff(st, 0, k)
        p1[k] = jnp.where(rows_ok, scale * d, 0.0)
    strip = sth[...]
    edges = pack([st[2 * levels + k] for k in range(levels)], spans[0:levels], lane)
    r, l = strip_sides(pltpu.roll(strip, 128 - 2 * span_f, 1), edges)
    one = pltpu.roll(strip, 128 - span_f, 1)
    up, down = strip_levels(strip)
    d = next_row(one) - prev_row(one) + inv_s[...] * (r - l) + (up - down)
    p1h[...] = jnp.where(halo_ok & (lane < span_f), scale * d, 0.0)

    shape = mine.shape
    place = lax.broadcasted_iota(jnp.int32, shape, 0) * 128
    place = place + lax.broadcasted_iota(jnp.int32, shape, 1)
    tile = jnp.zeros(shape, F32)
    for k in range(levels):
        part = coef_a[...] * p1[k] + jnp.where(lane // 6 == k, coef_h[...] * p1h[...], 0.0)
        part = part + jnp.where(is_own, levels_sum(p1, 0, k), 0.0)
        total = jnp.sum(jnp.sum(part, axis=0, keepdims=True), axis=1, keepdims=True)
        tile = tile + jnp.where(place == me * levels + k, total * (1.0 / 128.0), 0.0)
    mine[...] = tile

    def sum_copy(t, there, i):
        return pltpu.make_async_remote_copy(
            src_ref=mine, dst_ref=sums.at[there],
            send_sem=sum_send.at[i], recv_sem=sum_recv.at[there],
            device_id=dev(p, t // n_lon, lax.rem(t, n_lon)), device_id_type=MESH,
        )

    def send_sum(i, carry):
        sum_copy(lax.rem(me + i, ndev), me, i).start()
        return carry

    lax.fori_loop(1, ndev, send_sum, 0)

    gain_o = gain_s[own, :]
    inv_o = inv_s[own, :]
    first_o, last_o = lane_o == 0, lane_o == 127

    halo_wait_recv(hargs[1])
    unpack_rows(GROUPS[1], hargs[1])
    spans2 = windows(levels, GROUPS[1])
    merged2 = jnp.where(right_part(spans2, lane_o), pkr2[...], pkl2[...])
    for f in range(3, 6):
        for k in range(levels):
            c = f * levels + k
            body = x[c]
            mid = body[TOP : TOP + 128]
            if f == 3:
                r, l = sides(mid, hx[own, :], spans[c][0], first_o, last_o)
            else:
                r, l = sides(mid, merged2, spans2[c - 4 * levels][0], first_o, last_o)
            lap = next_row(body)[TOP : TOP + 128] + prev_row(body)[TOP : TOP + 128]
            lap = lap + gain_o * (r + l) - (4.0 + 2.0 * gain_o) * mid
            lap = lap + levels_sum(x, f * levels, k, own)
            onew[f, k] = mid + va[k, own, :] * lap
    store_late = pltpu.make_async_copy(
        onew.at[pl.ds(3, 3)], out_ref.at[pl.ds(3, 3)], out_sem.at[0]
    )
    store_late.start()
    for k in range(levels):
        body = p1[k]
        mid = body[TOP : TOP + 128]
        r, l = sides(mid, p1h[own, :], spans[k][0], first_o, last_o)
        diff = next_row(body)[TOP : TOP + 128] - prev_row(body)[TOP : TOP + 128]
        onew[0, k] = st[k, own, :] - 0.5 * levels_diff(p1, 0, k, own)
        onew[1, k] = st[levels + k, own, :] - 0.5 * diff
        onew[2, k] = st[2 * levels + k, own, :] - 0.5 * inv_o * (r - l)

    store_new = pltpu.make_async_copy(
        onew.at[pl.ds(0, 3)], out_ref.at[pl.ds(0, 3)], out_sem.at[1]
    )
    store_p = pltpu.make_async_copy(p1.at[:, own, :], press_ref, out_sem.at[2])
    store_new.start()
    store_p.start()

    for c in load_o:
        c.wait()

    def take_sum(i, total):
        s = lax.rem(me + i, ndev)
        sum_copy(me, s, 0).wait_recv()
        return total + sums[s]

    vec = lax.fori_loop(1, ndev, take_sum, mine[...])

    def coarse(t, k):
        prod = opr[t, k] * vec
        return jnp.sum(jnp.sum(prod, axis=0, keepdims=True), axis=1, keepdims=True)

    zero = jnp.zeros((1, 1), F32)
    there = (None, a > 0, a < n_lat - 1, b > 0, b < n_lon - 1)
    for t in range(5):
        for k in range(levels):
            c = coarse(t, k)
            c = c if t == 0 else jnp.where(there[t], c, zero)
            cvals[t * levels + k : t * levels + k + 1, :] = jnp.broadcast_to(c, (1, 128))
    store_c = pltpu.make_async_copy(cvals, cv_ref, out_sem.at[3])
    store_c.start()

    def end_lon(q, carry):
        ask_copy(q, b).wait_send()
        rep_copy(0, q, b).wait_send()
        rep_copy(1, q, b).wait_send()
        return carry

    lax.fori_loop(0, n_lon, end_lon, 0)
    halo_wait_send(vargs)
    halo_wait_send(hargs[0])
    halo_wait_send(hargs[1])

    def end_sum(i, carry):
        sum_copy(me, me, i).wait_send()
        return carry

    lax.fori_loop(1, ndev, end_sum, 0)
    store_late.wait()
    store_new.wait()
    store_p.wait()
    store_c.wait()


def finish(
    dims, part_f, part_p, cv_in, out_ref, press_ref, new, press, cvals, in_sem, out_sem
):
    n_lat, levels = dims
    a = lax.axis_index("lat")
    late, early = pl.ds(3, 3), pl.ds(0, 3)
    loads = [
        pltpu.make_async_copy(src, dst, in_sem.at[i])
        for i, (src, dst) in enumerate(
            (
                (part_f.at[late], new.at[late]), (part_f.at[early], new.at[early]),
                (part_p, press), (cv_in, cvals),
            )
        )
    ]
    for c in loads:
        c.start()
    row = lax.broadcasted_iota(jnp.int32, (128, 128), 0)
    lane = lax.broadcasted_iota(jnp.int32, (128, 128), 1)
    colat = math.pi / 4.0 + ((a * 128 + row).astype(F32) + 0.5) * (math.pi / 2.0) / (
        n_lat * 128
    )
    inv = 1.0 / jnp.sin(colat)
    stores = [
        pltpu.make_async_copy(new.at[late], out_ref.at[0, late], out_sem.at[0]),
        pltpu.make_async_copy(new.at[early], out_ref.at[0, early], out_sem.at[1]),
        pltpu.make_async_copy(press, press_ref.at[0], out_sem.at[2]),
    ]
    loads[0].wait()
    stores[0].start()
    for c in loads[1:]:
        c.wait()

    def value(t, k):
        at = t * levels + k
        return cvals[at : at + 1, :]

    for k in range(levels):
        c = value(0, k)
        press[k] = press[k] + c
        high = value(0, k + 1) if k + 1 < levels else 0.0
        low = value(0, k - 1) if k > 0 else 0.0
        new[0, k] = new[0, k] - 0.5 * (high - low)
        fix = jnp.where(row == 0, c - value(1, k), 0.0)
        fix = jnp.where(row == 127, value(2, k) - c, fix)
        new[1, k] = new[1, k] - 0.5 * fix
        fix = jnp.where(lane == 0, c - value(3, k), 0.0)
        fix = jnp.where(lane == 127, value(4, k) - c, fix)
        new[2, k] = new[2, k] - 0.5 * inv * fix
    stores[1].start()
    stores[2].start()
    for c in stores:
        c.wait()


def solution(mesh):
    n_lat, n_lon = mesh.shape["lat"], mesh.shape["lon"]

    def shards(fields, viscosity, partner, src_row, src_col, weight_id, border_angle, dest_cell):
        levels = fields.shape[2]
        blocks = partner.shape[2]
        channels = 6 * levels
        ext = 128 + 2 * TOP
        ndev = n_lat * n_lon
        cells = src_row.shape[2]
        oper = jnp.asarray(coarse_operator(levels, n_lat, n_lon))
        anyw = pl.BlockSpec(memory_space=pl.ANY)
        v = lambda *s: pltpu.VMEM(s, F32)
        vi = lambda *s: pltpu.VMEM(s, jnp.int32)
        sem = lambda n: pltpu.SemaphoreType.DMA((n,))
        rows0, rows1 = 12 * levels, 2 * levels
        used = oper.shape[2]
        part_f, part_p, cvals = pl.pallas_call(
            functools.partial(kernel, (n_lat, n_lon, levels, blocks)),
            out_shape=(
                jax.ShapeDtypeStruct(fields.shape[1:], F32),
                jax.ShapeDtypeStruct(viscosity.shape[1:], F32),
                jax.ShapeDtypeStruct((5 * levels, 128), F32),
            ),
            in_specs=[anyw] * 9,
            out_specs=(anyw, anyw, anyw),
            scratch_shapes=[
                vi(1, 1, blocks), vi(1, 1, cells), vi(1, 1, cells), vi(1, 1, cells),
                v(1, 1, cells), vi(1, 1, cells),
                v(6, levels, 128, 128),
                pltpu.VMEM((6, levels * 128, 256), BF16),
                vi(n_lon, 4, 128), vi(n_lon, 4, 128),
                v(n_lon, 4 * levels, 128), v(n_lon, 4 * levels, 128),
                v(n_lon, 2 * levels, 128), v(n_lon, 2 * levels, 128),
                v(channels, ext, 128),
                v(ext, 128),
                v(128, 128), v(ext, 128), v(ext, 128),
                v(128, 128), v(128, 128), v(128, 128),
                v(rows0, 128), v(rows0, 128), v(rows0, 128), v(rows0, 128),
                v(rows1, 128), v(rows1, 128), v(rows1, 128), v(rows1, 128),
                v(levels, ext, 128), v(ext, 128),
                v(128, 128), v(ext, 128), v(ext, 128),
                v(ext, 128), v(ext, 128), v(ext, 128), v(ext, 128),
                v(3 * levels, ext, 128), v(ext, 128),
                v(levels, ext, 128), v(ext, 128),
                v(128, 128),
                pltpu.VMEM((128, cells), BF16),
                pltpu.VMEM((128, 2 * cells), BF16),
                v(5, levels, used, 128),
                v(ndev, used, 128),
                v(used, 128),
                v(6, levels, 128, 128),
                v(5 * levels, 128),
                sem(8), sem(5), sem(4),
                sem(n_lon), sem(n_lon), sem(2 * n_lon), sem(2 * n_lon),
                sem(8), sem(8), sem(8), sem(8), sem(8), sem(8), sem(ndev), sem(ndev),
            ],
            compiler_params=pltpu.CompilerParams(
                collective_id=0, has_side_effects=True, vmem_limit_bytes=60 * 1024 * 1024
            ),
            name="shell_step",
        )(
            partner.reshape(1, 1, blocks), src_row, src_col, weight_id, border_angle, dest_cell,
            fields, viscosity, oper,
        )
        return pl.pallas_call(
            functools.partial(finish, (n_lat, levels)),
            out_shape=(
                jax.ShapeDtypeStruct(fields.shape, F32),
                jax.ShapeDtypeStruct(viscosity.shape, F32),
            ),
            in_specs=[anyw] * 3,
            out_specs=(anyw, anyw),
            scratch_shapes=[
                v(6, levels, 128, 128), v(levels, 128, 128), v(5 * levels, 128), sem(4), sem(3),
            ],
            compiler_params=pltpu.CompilerParams(vmem_limit_bytes=60 * 1024 * 1024),
            name="finish",
        )(part_f, part_p, cvals)

    return jax.shard_map(
        shards,
        mesh=mesh,
        in_specs=(
            P("panel", None, None, "lat", "lon"),
            P("panel", None, "lat", "lon"),
            P("panel", "lat", "lon", None),
            P("panel", "lat", "lon"),
            P("panel", "lat", "lon"),
            P("panel", "lat", "lon"),
            P("panel", "lat", "lon"),
            P("panel", "lat", "lon"),
        ),
        out_specs=(P("panel", None, None, "lat", "lon"), P("panel", None, "lat", "lon")),
        check_vma=False,
    )
```

```python
import functools
import math

import jax
import jax.numpy as jnp
import numpy as np
from jax import lax
from jax.experimental import pallas as pl
from jax.experimental.pallas import tpu as pltpu
from jax.sharding import PartitionSpec as P

MESH = pl.DeviceIdType.MESH
WQ = 8
BUOYANCY = 0.5
TOP = 8
F32 = jnp.float32
BF16 = jnp.bfloat16


def coarse_operator(levels, n_lat, n_lon):
    def table(n):
        m = np.arange(n, dtype=np.float64)
        norm = np.sqrt(np.where(m > 0, 2.0, 1.0) / n)
        q = norm[:, None] * np.cos(np.pi * m[:, None] * (m[None, :] + 0.5) / n)
        return q, 4.0 * np.sin(np.pi * m / (2.0 * n)) ** 2

    qr, er = table(levels)
    qa, ea = table(n_lat)
    qo, eo = table(n_lon)
    inv = 1.0 / (
        ea[:, None, None] + eo[None, :, None] + er[None, None, :] + 1.0 / (n_lat * n_lon)
    )
    q = np.einsum("ax,oy,rz->aorxyz", qa, qo, qr).reshape(inv.size, inv.size)
    full = (q.T * inv.reshape(-1)) @ q / math.sqrt(n_lat * n_lon)
    count = inv.size
    used = -(-count // 128)
    wide = np.zeros((count, used * 128), np.float32)
    wide[:, :count] = full
    return wide.reshape(n_lat * n_lon, levels, used, 128)


def short_loop(start, end, body, init):
    return lax.fori_loop(start, end, body, init, unroll=end - start <= 16)


GROUPS = ((0, 4), (4, 6))
WIDTHS = (3, 3, 3, 3, 1, 1)


def windows(levels, group):
    spans, at = [], 0
    for width in WIDTHS[group[0] : group[1]]:
        for _ in range(levels):
            spans.append((at + width, width))
            at += 2 * width
    return spans


def visc_windows(levels):
    return [(6 * k + 3, 3) for k in range(levels)]


def pack(tiles, spans, lane):
    packed = None
    for tile, (centre, width) in zip(tiles, spans):
        moved = pltpu.roll(tile, centre, 1)
        inside = (lane >= centre - width) & (lane < centre + width)
        packed = jnp.where(inside, moved, 0.0 if packed is None else packed)
    return packed


def right_part(spans, lane):
    mask = jnp.zeros(lane.shape, jnp.int32)
    for centre, width in spans:
        mask = jnp.where((lane >= centre) & (lane < centre + width), 1, mask)
    return mask > 0


def kernel(
    dims,
    partner_in, row_in, col_in, wid_in, ang_in, dest_in, fields_ref, visc_ref, oper_ref,
    out_ref, press_ref, cv_ref,
    partner_ref, row_ref, col_ref, wid_ref, ang_ref, dest_ref,
    fld, fcat, ask, asked, reply0, answer0, reply1, answer1, x, hx,
    pk, pkl, pkr, pk2, pkl2, pkr2, to_up, to_dn, from_up, from_dn,
    to_up2, to_dn2, from_up2, from_dn2, va, vh, vpk, vpl, vpr,
    inv_s, gain_s, coef_a, coef_h, st, sth, p1, p1h, hit_s, rmask, cmask,
    opr, sums, mine, onew, cvals,
    in_sem, op_sem, out_sem, ask_send, ask_recv, rep_send, rep_recv,
    halo_send, halo_recv, halo2_send, halo2_recv, v_send, v_recv, sum_send, sum_recv,
):
    n_lat, n_lon, levels, blocks = dims
    ndev = n_lat * n_lon
    channels = 6 * levels
    rows_ext = 128 + 2 * TOP
    pairs = blocks // 2
    cells = blocks * 64
    p = lax.axis_index("panel")
    a = lax.axis_index("lat")
    b = lax.axis_index("lon")
    me = a * n_lon + b
    own = pl.ds(TOP, 128)

    def dev(panel, lat, lon):
        return {"panel": panel, "lat": lat, "lon": lon}

    load_f = pltpu.make_async_copy(fields_ref.at[0], fld, in_sem.at[0])
    load_v = pltpu.make_async_copy(visc_ref.at[0], va.at[:, own, :], in_sem.at[1])
    small = [
        pltpu.make_async_copy(src, dst, in_sem.at[2 + i])
        for i, (src, dst) in enumerate(
            (
                (partner_in, partner_ref), (row_in, row_ref), (col_in, col_ref),
                (wid_in, wid_ref), (ang_in, ang_ref), (dest_in, dest_ref),
            )
        )
    ]
    for c in small:
        c.start()
    load_f.start()
    load_v.start()
    targets = (
        me,
        jnp.maximum(a - 1, 0) * n_lon + b,
        jnp.minimum(a + 1, n_lat - 1) * n_lon + b,
        a * n_lon + jnp.maximum(b - 1, 0),
        a * n_lon + jnp.minimum(b + 1, n_lon - 1),
    )
    load_o = [
        pltpu.make_async_copy(oper_ref.at[t], opr.at[i], op_sem.at[i])
        for i, t in enumerate(targets)
    ]
    for c in load_o:
        c.start()

    barrier = pltpu.get_barrier_semaphore()

    def greet(i, carry):
        t = lax.rem(me + i, ndev)
        pl.semaphore_signal(
            barrier, inc=1, device_id=dev(p, t // n_lon, lax.rem(t, n_lon)), device_id_type=MESH
        )
        return carry

    short_loop(1, ndev, greet, 0)

    def greet_other(i, carry):
        pl.semaphore_signal(barrier, inc=1, device_id=dev(1 - p, a, i), device_id_type=MESH)
        return carry

    short_loop(0, n_lon, greet_other, 0)

    lane8 = lax.broadcasted_iota(jnp.int32, (8, 128), 1)
    sub8 = lax.broadcasted_iota(jnp.int32, (8, 128), 0)
    half = lane8 // 64
    zero_rows = jnp.zeros((6 * levels, TOP, 128), F32)
    x[:, 0:TOP, :] = zero_rows
    x[:, TOP + 128 : rows_ext, :] = zero_rows
    for c in small[:4]:
        c.wait()
    named = jnp.broadcast_to(partner_ref[0], (blocks, blocks)).astype(F32)
    diag = lax.broadcasted_iota(jnp.int32, (blocks, blocks), 0) == lax.broadcasted_iota(
        jnp.int32, (blocks, blocks), 1
    )
    pv = jnp.sum(jnp.where(diag, named, 0.0), axis=1, keepdims=True).astype(jnp.int32)
    pv = jnp.broadcast_to(pv, (blocks, 128))
    block_id = lax.broadcasted_iota(jnp.int32, (blocks, 128), 0)
    before = jnp.zeros((blocks, 128), jnp.int32)
    for k in range(blocks):
        before = before + jnp.where((pv == pv[k : k + 1]) & (block_id > k), 1, 0)
    slot = pv * 2 + before
    keys, keys_r, tiles, tiles_r = [], [], [], []
    for j in range(pairs):
        s0 = jnp.broadcast_to(slot[2 * j : 2 * j + 1], (8, 128))
        s1 = jnp.broadcast_to(slot[2 * j + 1 : 2 * j + 2], (8, 128))
        key = jnp.where(half == 0, s0, s1)
        at = pl.ds(128 * j, 128)
        rr = jnp.broadcast_to(row_ref[0, :, at], (8, 128))
        cc = jnp.broadcast_to(col_ref[0, :, at], (8, 128))
        ww = jnp.broadcast_to(wid_ref[0, :, at], (8, 128))
        tile = jnp.where(sub8 == 0, rr, jnp.where(sub8 == 1, cc, ww))
        keys.append(key)
        tiles.append(tile)
        keys_r.append(pltpu.roll(key, 64, 1))
        tiles_r.append(pltpu.roll(tile, 64, 1))
    for q in range(n_lon):
        want = 2 * q + half
        acc = jnp.zeros((8, 128), jnp.int32)
        for j in range(pairs):
            acc = jnp.where(keys[j] == want, tiles[j], acc)
            acc = jnp.where(keys_r[j] == want, tiles_r[j], acc)
        ask[q] = acc[0:4]

    pl.semaphore_wait(barrier, ndev - 1 + n_lon)

    def ask_copy(q, there):
        return pltpu.make_async_remote_copy(
            src_ref=ask.at[q], dst_ref=asked.at[there],
            send_sem=ask_send.at[q], recv_sem=ask_recv.at[there],
            device_id=dev(1 - p, a, q), device_id_type=MESH,
        )

    def send_ask(i, carry):
        q = lax.rem(b + i, n_lon)
        ask_copy(q, b).start()
        return carry

    short_loop(0, n_lon, send_ask, 0)

    ways = [(da, db) for da in (-1, 0, 1) for db in (-1, 0, 1) if (da, db) != (0, 0)]

    def exists(da, db):
        ok = None
        for pos, d, n in ((a, da, n_lat), (b, db, n_lon)):
            if d:
                c = (pos > 0) if d < 0 else (pos < n - 1)
                ok = c if ok is None else jnp.logical_and(ok, c)
        return ok

    def halo_copy(w, h):
        da, db = ways[w]
        src_rows = {-1: pl.ds(0, TOP), 0: pl.ds(0, 128), 1: pl.ds(128 - TOP, TOP)}[da]
        dst_rows = {-1: pl.ds(TOP + 128, TOP), 0: own, 1: pl.ds(0, TOP)}[da]
        if db == 0 and h["rows"] is not None:
            up, dn, got_up, got_dn = h["rows"]
            src, dst = (up, got_dn) if da < 0 else (dn, got_up)
        elif db == 0:
            src = h["body"].at[:, pl.ds(TOP if da < 0 else 128, TOP), :]
            dst = h["body"].at[:, dst_rows, :]
        else:
            into = h["cols"][1 if db > 0 else 2]
            src = h["cols"][0].at[src_rows, :]
            dst = into if h["flat"] else into.at[dst_rows, :]
        return pltpu.make_async_remote_copy(
            src_ref=src, dst_ref=dst, send_sem=h["send"].at[w], recv_sem=h["recv"].at[w],
            device_id=dev(p, a + da, b + db), device_id_type=MESH,
        )

    def ways_of(h):
        return [w for w, (da, db) in enumerate(ways) if not (h["flat"] and da and db)]

    def halo_send_all(h):
        for w in ways_of(h):
            @pl.when(exists(*ways[w]))
            def _(w=w):
                halo_copy(w, h).start()

    def halo_wait_recv(h):
        for w in ways_of(h):
            da, db = ways[w]

            @pl.when(exists(-da, -db))
            def _(w=w):
                halo_copy(w, h).wait_recv()

    def halo_wait_send(h):
        for w in ways_of(h):
            @pl.when(exists(*ways[w]))
            def _(w=w):
                halo_copy(w, h).wait_send()

    def halo_clear(h):
        for w in ways_of(h):
            da, db = ways[w]
            dst_rows = {-1: pl.ds(TOP + 128, TOP), 0: own, 1: pl.ds(0, TOP)}[da]
            if db == 0 and h["rows"] is not None:
                continue

            @pl.when(jnp.logical_not(exists(-da, -db)))
            def _(da=da, db=db, dst_rows=dst_rows):
                if db == 0:
                    h["body"][:, dst_rows, :] = jnp.zeros((levels, TOP, 128), F32)
                else:
                    buf = h["cols"][1 if db > 0 else 2]
                    if h["flat"]:
                        buf[...] = jnp.zeros((128, 128), F32)
                    else:
                        buf[dst_rows, :] = jnp.zeros((128 if da == 0 else TOP, 128), F32)

    def rows_of(group):
        spots, at = [], 0
        for f in range(*group):
            for k in range(levels):
                spots.append((f * levels + k, at, WIDTHS[f]))
                at += WIDTHS[f]
        return spots

    def pack_rows(group, h):
        up, dn = h["rows"][0:2]

        @pl.when(a > 0)
        def _():
            for c, at, w in rows_of(group):
                up[at : at + w, :] = x[c, TOP : TOP + w, :]

        @pl.when(a < n_lat - 1)
        def _():
            for c, at, w in rows_of(group):
                dn[at : at + w, :] = x[c, TOP + 128 - w : TOP + 128, :]

    def unpack_rows(group, h):
        got_up, got_dn = h["rows"][2:4]

        @pl.when(a > 0)
        def _():
            for c, at, w in rows_of(group):
                x[c, TOP - w : TOP, :] = got_up[at : at + w, :]

        @pl.when(a < n_lat - 1)
        def _():
            for c, at, w in rows_of(group):
                x[c, TOP + 128 : TOP + 128 + w, :] = got_dn[at : at + w, :]

    lane = lax.broadcasted_iota(jnp.int32, (rows_ext, 128), 1)
    lane_o = lax.broadcasted_iota(jnp.int32, (128, 128), 1)
    row_e = lax.broadcasted_iota(jnp.int32, (rows_ext, 128), 0)

    vargs = dict(
        rows=None, body=va, cols=(vpk, vpl, vpr), flat=False, send=v_send, recv=v_recv
    )
    hargs = (
        dict(
            rows=(to_up, to_dn, from_up, from_dn), cols=(pk, pkl, pkr), flat=False,
            send=halo_send, recv=halo_recv,
        ),
        dict(
            rows=(to_up2, to_dn2, from_up2, from_dn2), cols=(pk2, pkl2, pkr2), flat=True,
            send=halo2_send, recv=halo2_recv,
        ),
    )
    halo_clear(vargs)
    load_v.wait()
    vpk[...] = pack([va[k, own, :] for k in range(levels)], visc_windows(levels), lane_o)
    halo_send_all(vargs)
    halo_clear(hargs[0])
    halo_clear(hargs[1])

    load_f.wait()
    for f in range(6):
        v = fld[f].reshape(levels * 128, 128)
        hi = v.astype(BF16)
        lo = (v - hi.astype(F32)).astype(BF16)
        fcat[f, :, 0:128] = hi
        fcat[f, :, 128:256] = lo

    small[4].wait()
    cos_a = jnp.cos(ang_ref[0])
    sin_a = jnp.sin(ang_ref[0])
    colat = math.pi / 4.0 + ((a * 128 + row_e - TOP).astype(F32) + 0.5) * (
        math.pi / 2.0
    ) / (n_lat * 128)
    inv = 1.0 / jnp.sin(colat)
    gain = inv * inv
    inv_s[...] = inv
    gain_s[...] = gain
    is_own = (row_e >= TOP) & (row_e < TOP + 128)
    edge_lane = (lane == 0) | (lane == 127)
    ca = 2.0 + 2.0 * gain
    ca = ca - jnp.where((row_e == TOP) | (row_e == TOP + 127), 1.0, 0.0)
    ca = ca - jnp.where(edge_lane, gain, 0.0)
    rim = jnp.where((row_e == TOP - 1) | (row_e == TOP + 128), 1.0, 0.0)
    coef_a[...] = jnp.where(is_own, ca, rim)
    slot6 = lane % 6
    at_west, at_east = slot6 == 2, slot6 == 3
    coef_h[...] = jnp.where(is_own & (at_west | at_east), gain, 0.0)

    replies, answers = (reply0, reply1), (answer0, answer1)

    def rep_copy(g, q, there):
        return pltpu.make_async_remote_copy(
            src_ref=replies[g].at[q], dst_ref=answers[g].at[there],
            send_sem=rep_send.at[g * n_lon + q], recv_sem=rep_recv.at[g * n_lon + there],
            device_id=dev(1 - p, a, q), device_id_type=MESH,
        )

    sub_c = lax.broadcasted_iota(jnp.int32, (128, 256), 0)

    def serve(g, i, carry):
        pr = lax.rem(b // 2 + i, n_lon // 2)
        q0 = 2 * pr
        if g == 0:
            ask_copy(0, q0).wait_recv()
            ask_copy(0, q0 + 1).wait_recv()
        r0 = asked[q0]
        r1 = asked[q0 + 1]
        rr = jnp.concatenate([r0[0:1], r1[0:1]], axis=1)
        cc = jnp.concatenate([r0[1:2], r1[1:2]], axis=1)
        ww = jnp.concatenate([r0[2:3], r1[2:3]], axis=1)
        fa = ((ww >> 3).astype(F32) + 0.5) / WQ
        fo = ((ww & 7).astype(F32) + 0.5) / WQ
        cw = jnp.where(sub_c == cc, 1.0 - fo, jnp.where(sub_c == cc + 1, fo, 0.0)).astype(BF16)
        rw = jnp.where(sub_c == rr, 1.0 - fa, jnp.where(sub_c == rr + 1, fa, 0.0))
        cw2 = jnp.concatenate([cw, cw], axis=0)
        parts = []
        for f in range(*GROUPS[g]):
            v = jnp.dot(fcat[f], cw2, preferred_element_type=F32)
            parts.append(jnp.sum(v.reshape(levels, 128, 256) * rw[None], axis=1))
        res = jnp.concatenate(parts, axis=0)
        replies[g][q0] = res[:, 0:128]
        replies[g][q0 + 1] = res[:, 128:256]
        rep_copy(g, q0, b).start()
        rep_copy(g, q0 + 1, b).start()
        return carry

    lax.fori_loop(0, n_lon // 2, functools.partial(serve, 0), 0)
    small[5].wait()
    dest = dest_ref[0]
    sub_d = lax.broadcasted_iota(jnp.int32, (128, cells), 0)
    rm = jnp.where(sub_d == dest // 128, 1.0, 0.0).astype(BF16)
    cm = jnp.where(sub_d == dest % 128, 1.0, 0.0).astype(BF16)
    rmask[...] = rm
    cmask[:, 0:cells] = cm
    cmask[:, cells : 2 * cells] = cm
    nt = (((1,), (1,)), ((), ()))
    hit_s[...] = lax.dot_general(rm, cm, nt, preferred_element_type=F32)
    lax.fori_loop(0, n_lon // 2, functools.partial(serve, 1), 0)
    halo_wait_recv(vargs)
    vmerged = jnp.where(right_part(visc_windows(levels), lane), vpr[...], vpl[...])
    span_f = 6 * levels
    vh[...] = jnp.where(
        lane < span_f, vmerged,
        jnp.where(
            lane < 2 * span_f, pltpu.roll(vmerged, span_f, 1), pltpu.roll(vmerged, 2 * span_f, 1)
        ),
    )

    half_row = half[0:1]

    def fill(g):
        first_f, end_f = GROUPS[g]

        def wait_rep(q, carry):
            rep_copy(g, 0, q).wait_recv()
            return carry

        short_loop(0, n_lon, wait_rep, 0)
        got = [answers[g][q] for q in range(n_lon)]
        got_r = [pltpu.roll(v, 64, 1) for v in got]
        picked = []
        for j in range(pairs):
            key = keys[j][0:1]
            acc = jnp.zeros(((end_f - first_f) * levels, 128), F32)
            for q in range(n_lon):
                acc = jnp.where(key == 2 * q + half_row, got[q], acc)
                acc = jnp.where(key == 2 * q + 1 - half_row, got_r[q], acc)
            picked.append(acc)
        values = jnp.concatenate(picked, axis=1)
        fv = [values[f * levels : (f + 1) * levels] for f in range(end_f - first_f)]
        if g == 0:
            turned = [
                fv[0], cos_a * fv[1] + sin_a * fv[2], cos_a * fv[2] - sin_a * fv[1], fv[3],
            ]
        else:
            turned = [cos_a * fv[0] + sin_a * fv[1], cos_a * fv[1] - sin_a * fv[0]]
        hit = hit_s[...] > 0.5
        for f in range(first_f, end_f):
            v = turned[f - first_f]
            hi = v.astype(BF16)
            lo = (v - hi.astype(F32)).astype(BF16)
            left = []
            for k in range(levels):
                left.append(
                    jnp.concatenate(
                        [rmask[...] * hi[k : k + 1], rmask[...] * lo[k : k + 1]], axis=1
                    )
                )
            put = lax.dot_general(
                jnp.concatenate(left, axis=0), cmask[...], nt, preferred_element_type=F32
            )
            for k in range(levels):
                x[f * levels + k, own, :] = jnp.where(
                    hit, put[k * 128 : (k + 1) * 128], fld[f, k]
                )
        h = hargs[g]
        pack_rows(GROUPS[g], h)
        h["cols"][0][...] = pack(
            [x[c, own, :] for c in range(first_f * levels, end_f * levels)],
            windows(levels, GROUPS[g]), lane_o,
        )
        halo_send_all(h)

    fill(0)
    fill(1)
    halo_wait_recv(hargs[0])
    unpack_rows(GROUPS[0], hargs[0])
    spans = windows(levels, GROUPS[0])
    merged = jnp.where(right_part(spans, lane), pkr[...], pkl[...])
    hx[...] = merged
    own_edges = jnp.concatenate(
        [
            pack([x[c, 0:TOP, :] for c in range(4 * levels)], spans, lane8),
            pk[...],
            pack([x[c, TOP + 128 : rows_ext, :] for c in range(4 * levels)], spans, lane8),
        ],
        axis=0,
    )

    rows_ok = ((row_e >= TOP) | (a > 0)) & ((row_e < TOP + 128) | (a < n_lat - 1))
    lanes_ok = ((slot6 >= 3) | (b > 0)) & ((slot6 < 3) | (b < n_lon - 1))
    halo_ok = rows_ok & lanes_ok
    level = (lane // 6) % levels
    first, last = lane == 0, lane == 127

    def sides(body, strip, centre, at_first, at_last):
        r = jnp.where(
            at_last, pltpu.roll(strip, (127 - centre) % 128, 1), pltpu.roll(body, 127, 1)
        )
        l = jnp.where(
            at_first, pltpu.roll(strip, (129 - centre) % 128, 1), pltpu.roll(body, 1, 1)
        )
        return r, l

    def strip_sides(strip, edges):
        r = jnp.where(at_west, pltpu.roll(edges, 127, 1), pltpu.roll(strip, 127, 1))
        l = jnp.where(at_east, pltpu.roll(edges, 1, 1), pltpu.roll(strip, 1, 1))
        return r, l

    def strip_levels(strip):
        up = jnp.where(level < levels - 1, pltpu.roll(strip, 122, 1), 0.0)
        down = jnp.where(level > 0, pltpu.roll(strip, 6, 1), 0.0)
        return up, down

    def next_row(v):
        return pltpu.roll(v, rows_ext - 1, 0)

    def prev_row(v):
        return pltpu.roll(v, 1, 0)

    def levels_sum(ref, base, k, index=slice(None)):
        total = None
        for d in (-1, 1):
            if 0 <= k + d < levels:
                v = ref[base + k + d, index, :]
                total = v if total is None else total + v
        return total

    def levels_diff(ref, base, k, index=slice(None)):
        up = ref[base + k + 1, index, :] if k + 1 < levels else 0.0
        down = ref[base + k - 1, index, :] if k > 0 else 0.0
        return up - down

    gain = gain_s[...]
    mid = 4.0 + 2.0 * gain
    for f in range(3):
        for k in range(levels):
            c = f * levels + k
            body = x[c]
            r, l = sides(body, hx[...], spans[c][0], first, last)
            lap = next_row(body) + prev_row(body) + gain * (r + l) - mid * body
            lap = lap + levels_sum(x, f * levels, k)
            new = body + va[k] * lap
            if f == 0:
                new = new + BUOYANCY * x[3 * levels + k]
            st[c] = jnp.where(rows_ok, new, 0.0)
    strip = hx[...]
    r, l = strip_sides(strip, own_edges)
    up, down = strip_levels(strip)
    lap = next_row(strip) + prev_row(strip) + gain * (r + l) - mid * strip + (up + down)
    new = strip + vh[...] * lap
    warm = pltpu.roll(strip, 128 - 3 * span_f, 1)
    new = new + jnp.where(lane < span_f, BUOYANCY * warm, 0.0)
    sth[...] = jnp.where(halo_ok & (lane < 3 * span_f), new, 0.0)

    scale = -0.5 / mid
    for k in range(levels):
        r, l = sides(st[2 * levels + k], sth[...], spans[2 * levels + k][0], first, last)
        b1 = st[levels + k]
        d = next_row(b1) - prev_row(b1) + inv_s[...] * (r - l) + levels_diff(st, 0, k)
        p1[k] = jnp.where(rows_ok, scale * d, 0.0)
    strip = sth[...]
    edges = pack([st[2 * levels + k] for k in range(levels)], spans[0:levels], lane)
    r, l = strip_sides(pltpu.roll(strip, 128 - 2 * span_f, 1), edges)
    one = pltpu.roll(strip, 128 - span_f, 1)
    up, down = strip_levels(strip)
    d = next_row(one) - prev_row(one) + inv_s[...] * (r - l) + (up - down)
    p1h[...] = jnp.where(halo_ok & (lane < span_f), scale * d, 0.0)

    shape = mine.shape
    place = lax.broadcasted_iota(jnp.int32, shape, 0) * 128
    place = place + lax.broadcasted_iota(jnp.int32, shape, 1)
    tile = jnp.zeros(shape, F32)
    for k in range(levels):
        part = coef_a[...] * p1[k] + jnp.where(lane // 6 == k, coef_h[...] * p1h[...], 0.0)
        part = part + jnp.where(is_own, levels_sum(p1, 0, k), 0.0)
        total = jnp.sum(jnp.sum(part, axis=0, keepdims=True), axis=1, keepdims=True)
        tile = tile + jnp.where(place == me * levels + k, total * (1.0 / 128.0), 0.0)
    mine[...] = tile

    def sum_copy(t, there, i):
        return pltpu.make_async_remote_copy(
            src_ref=mine, dst_ref=sums.at[there],
            send_sem=sum_send.at[i], recv_sem=sum_recv.at[there],
            device_id=dev(p, t // n_lon, lax.rem(t, n_lon)), device_id_type=MESH,
        )

    def send_sum(i, carry):
        sum_copy(lax.rem(me + i, ndev), me, i).start()
        return carry

    short_loop(1, ndev, send_sum, 0)

    gain_o = gain_s[own, :]
    inv_o = inv_s[own, :]
    first_o, last_o = lane_o == 0, lane_o == 127

    halo_wait_recv(hargs[1])
    unpack_rows(GROUPS[1], hargs[1])
    spans2 = windows(levels, GROUPS[1])
    merged2 = jnp.where(right_part(spans2, lane_o), pkr2[...], pkl2[...])
    for f in range(3, 6):
        for k in range(levels):
            c = f * levels + k
            body = x[c]
            mid = body[TOP : TOP + 128]
            if f == 3:
                r, l = sides(mid, hx[own, :], spans[c][0], first_o, last_o)
            else:
                r, l = sides(mid, merged2, spans2[c - 4 * levels][0], first_o, last_o)
            lap = next_row(body)[TOP : TOP + 128] + prev_row(body)[TOP : TOP + 128]
            lap = lap + gain_o * (r + l) - (4.0 + 2.0 * gain_o) * mid
            lap = lap + levels_sum(x, f * levels, k, own)
            onew[f, k] = mid + va[k, own, :] * lap
    store_late = pltpu.make_async_copy(
        onew.at[pl.ds(3, 3)], out_ref.at[pl.ds(3, 3)], out_sem.at[0]
    )
    store_late.start()
    for k in range(levels):
        body = p1[k]
        mid = body[TOP : TOP + 128]
        r, l = sides(mid, p1h[own, :], spans[k][0], first_o, last_o)
        diff = next_row(body)[TOP : TOP + 128] - prev_row(body)[TOP : TOP + 128]
        onew[0, k] = st[k, own, :] - 0.5 * levels_diff(p1, 0, k, own)
        onew[1, k] = st[levels + k, own, :] - 0.5 * diff
        onew[2, k] = st[2 * levels + k, own, :] - 0.5 * inv_o * (r - l)

    store_new = pltpu.make_async_copy(
        onew.at[pl.ds(0, 3)], out_ref.at[pl.ds(0, 3)], out_sem.at[1]
    )
    store_p = pltpu.make_async_copy(p1.at[:, own, :], press_ref, out_sem.at[2])
    store_new.start()
    store_p.start()

    for c in load_o:
        c.wait()

    def take_sum(i, total):
        s = lax.rem(me + i, ndev)
        sum_copy(me, s, 0).wait_recv()
        return total + sums[s]

    vec = short_loop(1, ndev, take_sum, mine[...])

    def coarse(t, k):
        prod = opr[t, k] * vec
        return jnp.sum(jnp.sum(prod, axis=0, keepdims=True), axis=1, keepdims=True)

    zero = jnp.zeros((1, 1), F32)
    there = (None, a > 0, a < n_lat - 1, b > 0, b < n_lon - 1)
    for t in range(5):
        for k in range(levels):
            c = coarse(t, k)
            c = c if t == 0 else jnp.where(there[t], c, zero)
            cvals[t * levels + k : t * levels + k + 1, :] = jnp.broadcast_to(c, (1, 128))
    store_c = pltpu.make_async_copy(cvals, cv_ref, out_sem.at[3])
    store_c.start()

    def end_lon(q, carry):
        ask_copy(q, b).wait_send()
        rep_copy(0, q, b).wait_send()
        rep_copy(1, q, b).wait_send()
        return carry

    short_loop(0, n_lon, end_lon, 0)
    halo_wait_send(vargs)
    halo_wait_send(hargs[0])
    halo_wait_send(hargs[1])

    def end_sum(i, carry):
        sum_copy(me, me, i).wait_send()
        return carry

    short_loop(1, ndev, end_sum, 0)
    store_late.wait()
    store_new.wait()
    store_p.wait()
    store_c.wait()


def finish(
    dims, part_f, part_p, cv_in, out_ref, press_ref, new, press, cvals, in_sem, out_sem
):
    n_lat, levels = dims
    a = lax.axis_index("lat")
    late, early = pl.ds(3, 3), pl.ds(0, 3)
    loads = [
        pltpu.make_async_copy(src, dst, in_sem.at[i])
        for i, (src, dst) in enumerate(
            (
                (part_f.at[late], new.at[late]), (part_f.at[early], new.at[early]),
                (part_p, press), (cv_in, cvals),
            )
        )
    ]
    for c in loads:
        c.start()
    row = lax.broadcasted_iota(jnp.int32, (128, 128), 0)
    lane = lax.broadcasted_iota(jnp.int32, (128, 128), 1)
    colat = math.pi / 4.0 + ((a * 128 + row).astype(F32) + 0.5) * (math.pi / 2.0) / (
        n_lat * 128
    )
    inv = 1.0 / jnp.sin(colat)
    stores = [
        pltpu.make_async_copy(new.at[late], out_ref.at[0, late], out_sem.at[0]),
        pltpu.make_async_copy(new.at[early], out_ref.at[0, early], out_sem.at[1]),
        pltpu.make_async_copy(press, press_ref.at[0], out_sem.at[2]),
    ]
    loads[0].wait()
    stores[0].start()
    for c in loads[1:]:
        c.wait()

    def value(t, k):
        at = t * levels + k
        return cvals[at : at + 1, :]

    for k in range(levels):
        c = value(0, k)
        press[k] = press[k] + c
        high = value(0, k + 1) if k + 1 < levels else 0.0
        low = value(0, k - 1) if k > 0 else 0.0
        new[0, k] = new[0, k] - 0.5 * (high - low)
        fix = jnp.where(row == 0, c - value(1, k), 0.0)
        fix = jnp.where(row == 127, value(2, k) - c, fix)
        new[1, k] = new[1, k] - 0.5 * fix
        fix = jnp.where(lane == 0, c - value(3, k), 0.0)
        fix = jnp.where(lane == 127, value(4, k) - c, fix)
        new[2, k] = new[2, k] - 0.5 * inv * fix
    stores[1].start()
    stores[2].start()
    for c in stores:
        c.wait()


def solution(mesh):
    n_lat, n_lon = mesh.shape["lat"], mesh.shape["lon"]

    def shards(fields, viscosity, partner, src_row, src_col, weight_id, border_angle, dest_cell):
        levels = fields.shape[2]
        blocks = partner.shape[2]
        channels = 6 * levels
        ext = 128 + 2 * TOP
        ndev = n_lat * n_lon
        cells = src_row.shape[2]
        oper = jnp.asarray(coarse_operator(levels, n_lat, n_lon))
        anyw = pl.BlockSpec(memory_space=pl.ANY)
        v = lambda *s: pltpu.VMEM(s, F32)
        vi = lambda *s: pltpu.VMEM(s, jnp.int32)
        sem = lambda n: pltpu.SemaphoreType.DMA((n,))
        rows0, rows1 = 12 * levels, 2 * levels
        used = oper.shape[2]
        part_f, part_p, cvals = pl.pallas_call(
            functools.partial(kernel, (n_lat, n_lon, levels, blocks)),
            out_shape=(
                jax.ShapeDtypeStruct(fields.shape[1:], F32),
                jax.ShapeDtypeStruct(viscosity.shape[1:], F32),
                jax.ShapeDtypeStruct((5 * levels, 128), F32),
            ),
            in_specs=[anyw] * 9,
            out_specs=(anyw, anyw, anyw),
            scratch_shapes=[
                vi(1, 1, blocks), vi(1, 1, cells), vi(1, 1, cells), vi(1, 1, cells),
                v(1, 1, cells), vi(1, 1, cells),
                v(6, levels, 128, 128),
                pltpu.VMEM((6, levels * 128, 256), BF16),
                vi(n_lon, 4, 128), vi(n_lon, 4, 128),
                v(n_lon, 4 * levels, 128), v(n_lon, 4 * levels, 128),
                v(n_lon, 2 * levels, 128), v(n_lon, 2 * levels, 128),
                v(channels, ext, 128),
                v(ext, 128),
                v(128, 128), v(ext, 128), v(ext, 128),
                v(128, 128), v(128, 128), v(128, 128),
                v(rows0, 128), v(rows0, 128), v(rows0, 128), v(rows0, 128),
                v(rows1, 128), v(rows1, 128), v(rows1, 128), v(rows1, 128),
                v(levels, ext, 128), v(ext, 128),
                v(128, 128), v(ext, 128), v(ext, 128),
                v(ext, 128), v(ext, 128), v(ext, 128), v(ext, 128),
                v(3 * levels, ext, 128), v(ext, 128),
                v(levels, ext, 128), v(ext, 128),
                v(128, 128),
                pltpu.VMEM((128, cells), BF16),
                pltpu.VMEM((128, 2 * cells), BF16),
                v(5, levels, used, 128),
                v(ndev, used, 128),
                v(used, 128),
                v(6, levels, 128, 128),
                v(5 * levels, 128),
                sem(8), sem(5), sem(4),
                sem(n_lon), sem(n_lon), sem(2 * n_lon), sem(2 * n_lon),
                sem(8), sem(8), sem(8), sem(8), sem(8), sem(8), sem(ndev), sem(ndev),
            ],
            compiler_params=pltpu.CompilerParams(
                collective_id=0, has_side_effects=True, vmem_limit_bytes=60 * 1024 * 1024
            ),
            name="shell_step",
        )(
            partner.reshape(1, 1, blocks), src_row, src_col, weight_id, border_angle, dest_cell,
            fields, viscosity, oper,
        )
        return pl.pallas_call(
            functools.partial(finish, (n_lat, levels)),
            out_shape=(
                jax.ShapeDtypeStruct(fields.shape, F32),
                jax.ShapeDtypeStruct(viscosity.shape, F32),
            ),
            in_specs=[anyw] * 3,
            out_specs=(anyw, anyw),
            scratch_shapes=[
                v(6, levels, 128, 128), v(levels, 128, 128), v(5 * levels, 128), sem(4), sem(3),
            ],
            compiler_params=pltpu.CompilerParams(vmem_limit_bytes=60 * 1024 * 1024),
            name="finish",
        )(part_f, part_p, cvals)

    return jax.shard_map(
        shards,
        mesh=mesh,
        in_specs=(
            P("panel", None, None, "lat", "lon"),
            P("panel", None, "lat", "lon"),
            P("panel", "lat", "lon", None),
            P("panel", "lat", "lon"),
            P("panel", "lat", "lon"),
            P("panel", "lat", "lon"),
            P("panel", "lat", "lon"),
            P("panel", "lat", "lon"),
        ),
        out_specs=(P("panel", None, None, "lat", "lon"), P("panel", None, "lat", "lon")),
        check_vma=False,
    )
```
